256 devices in a mesh: front: 64 (over z, y, core), blk: 4 (over x).
Axes of the slice: x: 4, y: 4, z: 8, core: 2. Of those that a mesh axis runs over, the one named last changes fastest.
Arguments:
- pivot_inverse_0: float32 [1024, 1024], P('front', 'blk'), may hold values from -1 to 2, as said below
- pivot_inverse_1: float32 [2048, 1024], P('front', 'blk'), may hold values from -1 to 2, as said below
- below_factor_1: float32 [1024, 1024], P('front', 'blk'), may hold values from -0.1875 to 0.1875
- selector_1: int32 [2, 4], replicated, may hold values from 0 to 7, as said below
- pivot_inverse_2: float32 [4096, 1024], P('front', 'blk'), may hold values from -1 to 2, as said below
- below_factor_2: float32 [4096, 1024], P('front', 'blk'), may hold values from -0.125 to 0.125
- selector_2: int32 [4, 8], replicated, may hold values from 0 to 11, as said below
- pivot_inverse_3: float32 [8192, 1024], P('front', 'blk'), may hold values from -1 to 2, as said below
- below_factor_3: float32 [12288, 1024], P('front', 'blk'), may hold values from -0.109375 to 0.109375
- selector_3: int32 [8, 12], replicated, may hold values from 0 to 15, as said below
Outputs:
- sigma_diag_0: float32 [1024, 1024], P('front', 'blk')
- sigma_diag_1: float32 [2048, 1024], P('front', 'blk')
- sigma_below_1: float32 [1024, 1024], P('front', 'blk')
- sigma_diag_2: float32 [4096, 1024], P('front', 'blk')
- sigma_below_2: float32 [4096, 1024], P('front', 'blk')
- sigma_diag_3: float32 [8192, 1024], P('front', 'blk')
- sigma_below_3: float32 [12288, 1024], P('front', 'blk')
The draws below stay inside these ranges and needn't reach their ends.
Inputs may be any that keep to these rules, and one draw needn't show every extreme that they name: `selector_1`: each row holds 4 distinct increasing block numbers of the root front's 8 blocks, always the first and the last. `selector_2`: each row holds 8 distinct increasing block numbers of its parent front's 12 blocks, always the first and the last. `selector_3`: each row holds 12 distinct increasing block numbers of its parent front's 16 blocks, always the first and the last. `pivot_inverse_0`: lower triangular in each front's 1024 x 1024 block; diagonal entries between 0.4 and 2.0, entries below the diagonal under 0.9 / sqrt(1024) in magnitude. `pivot_inverse_1`: lower triangular in each front's 1024 x 1024 block; diagonal entries between 0.4 and 2.0, entries below the diagonal under 0.9 / sqrt(1024) in magnitude. `pivot_inverse_2`: lower triangular in each front's 1024 x 1024 block; diagonal entries between 0.4 and 2.0, entries below the diagonal under 0.9 / sqrt(1024) in magnitude. `pivot_inverse_3`: lower triangular in each front's 1024 x 1024 block; diagonal entries between 0.4 and 2.0, entries below the diagonal under 0.9 / sqrt(1024) in magnitude.
All inputs are finite; a program needn't handle non-finite values.
Results may differ from the reference program's by a relative error of at most 0.00015.
Values sent between devices are 32-bit elements; how exact they have to be, the bound alone decides.
No kernel may reach another device: no remote copies, remote signals or barrier semaphores. Data moves between devices by JAX's collectives and lax.ppermute only.
A program may use at most 64 MiB of HBM per device.

```python
import math
import jax
import jax.numpy as jnp
from jax import lax

S = 1024
BLOCK = 128
UB1 = 4
UB2 = 8
UB3 = 12
U1 = 512
U2 = 1024
U3 = 1536
FB0 = 8
FB1 = 12
FB2 = 16


def inverse_draw(key, count):
    first, second = jax.random.split(jax.random.fold_in(key, 11))
    rows = jnp.arange(count * S, dtype=jnp.int32)[:, None] % S
    columns = jnp.arange(S, dtype=jnp.int32)[None, :]
    diagonal = jax.random.uniform(first, (count * S, 1), jnp.float32, 0.6, 1.6)
    noise = jnp.clip(0.5 * jax.random.normal(second, (count * S, S), jnp.float32), -0.9, 0.9)
    scaled = noise / math.sqrt(S)
    lower = jnp.where(columns < rows, scaled, jnp.float32(0.0))
    return (lower + jnp.where(columns == rows, diagonal, jnp.float32(0.0))).astype(jnp.float32)


def selector_draw(key, count, chosen, parent_blocks):
    keys = jax.random.split(jax.random.fold_in(key, 23), count)

    def single(inner):
        middle = jax.random.permutation(inner, parent_blocks - 2)[:chosen - 2].astype(jnp.int32) + 1
        first = jnp.zeros((1,), jnp.int32)
        final = jnp.full((1,), parent_blocks - 1, jnp.int32)
        return jnp.sort(jnp.concatenate([first, middle, final]))
    return jax.vmap(single)(keys).astype(jnp.int32)


def draw_pivot_inverse_0(key, part):
    key = jax.random.fold_in(key, 101)
    return inverse_draw(key, 1)


def draw_pivot_inverse_1(key, part):
    key = jax.random.fold_in(key, 102)
    return inverse_draw(key, 2)


def draw_pivot_inverse_2(key, part):
    key = jax.random.fold_in(key, 103)
    return inverse_draw(key, 4)


def draw_pivot_inverse_3(key, part):
    key = jax.random.fold_in(key, 104)
    return inverse_draw(key, 8)


def draw_selector_1(key, part):
    key = jax.random.fold_in(key, 201)
    return selector_draw(key, 2, UB1, FB0)


def draw_selector_2(key, part):
    key = jax.random.fold_in(key, 202)
    return selector_draw(key, 4, UB2, FB1)


def draw_selector_3(key, part):
    key = jax.random.fold_in(key, 203)
    return selector_draw(key, 8, UB3, FB2)


def block_levels(own_key, dims, cuts, least, high):
    gain = 1.0
    for axis_at, parts in cuts:
        heights = jax.random.uniform(jax.random.fold_in(jax.random.fold_in(own_key, 6), axis_at), (parts,), jnp.float32, least / len(cuts), high / len(cuts))
        gain = gain * jnp.repeat(jnp.exp(heights), dims[axis_at] // parts).reshape((-1,) + (1,) * (len(dims) - 1 - axis_at))
    return gain


def normal_values(rng, dims, deviation, limit, pieces=(), held_as=jnp.bfloat16):
    values = deviation * jax.random.normal(rng, dims, jnp.float32)
    if pieces:
        values = values * block_levels(rng, dims, pieces, -0.22, 0.18)
    return jnp.clip(values, -limit, limit).astype(held_as)


def setup_inputs(seed: int = 0) -> dict:
    splits = jax.random.split(jax.random.key(seed), 11)
    pivot_inverse_0 = draw_pivot_inverse_0(jax.random.fold_in(splits[10], 71), 0)
    pivot_inverse_1 = draw_pivot_inverse_1(jax.random.fold_in(splits[10], 71), 0)
    below_factor_1 = normal_values(splits[2], (2 * U1, S), (2 * U1) ** -0.5, 0.1875, ((0, 64), (1, 4)), jnp.float32)
    selector_1 = draw_selector_1(jax.random.fold_in(splits[10], 71), 0)
    pivot_inverse_2 = draw_pivot_inverse_2(jax.random.fold_in(splits[10], 71), 0)
    below_factor_2 = normal_values(splits[5], (4 * U2, S), (2 * U2) ** -0.5, 0.125, ((0, 64), (1, 4)), jnp.float32)
    selector_2 = draw_selector_2(jax.random.fold_in(splits[10], 71), 0)
    pivot_inverse_3 = draw_pivot_inverse_3(jax.random.fold_in(splits[10], 71), 0)
    below_factor_3 = normal_values(splits[8], (8 * U3, S), (2 * U3) ** -0.5, 0.109375, ((0, 64), (1, 4)), jnp.float32)
    selector_3 = draw_selector_3(jax.random.fold_in(splits[10], 71), 0)
    return {"pivot_inverse_0": pivot_inverse_0, "pivot_inverse_1": pivot_inverse_1, "below_factor_1": below_factor_1, "selector_1": selector_1, "pivot_inverse_2": pivot_inverse_2, "below_factor_2": below_factor_2, "selector_2": selector_2, "pivot_inverse_3": pivot_inverse_3, "below_factor_3": below_factor_3, "selector_3": selector_3}


def product(left, right):
    return jnp.dot(left, right, precision=lax.Precision.HIGHEST, preferred_element_type=jnp.float32)


def block_rows(selector):
    offsets = jnp.arange(BLOCK, dtype=jnp.int32)
    return (selector[:, :, None] * BLOCK + offsets[None, None, :]).reshape(selector.shape[0], -1).astype(jnp.int32)


def sweep_level(parent_fronts, selector, inverse, below_factor, width, keep_front):
    count = selector.shape[0]
    inverse = inverse.reshape(count, S, S)
    below_factor = below_factor.reshape(count, width, S)
    chosen = block_rows(selector)
    parents = (jnp.arange(count, dtype=jnp.int32) // 2).astype(jnp.int32)

    def single(pivot_inv, factor, rows, parent):
        whole = parent_fronts[parent]
        ancestor = jnp.take(jnp.take(whole, rows, axis=0), rows, axis=1)
        coupling = product(factor, pivot_inv)
        below = -product(ancestor, coupling)
        diagonal = product(pivot_inv.T, pivot_inv) - product(coupling.T, below)
        return diagonal, below, ancestor

    diagonal, below, ancestor = jax.vmap(single)(inverse, below_factor, chosen, parents)
    fronts = None
    if keep_front:
        upper = jnp.concatenate([diagonal, jnp.swapaxes(below, 1, 2)], axis=2)
        lower = jnp.concatenate([below, ancestor], axis=2)
        fronts = jnp.concatenate([upper, lower], axis=1)
    return diagonal.reshape(count * S, S), below.reshape(count * width, S), fronts


def reference(pivot_inverse_0, pivot_inverse_1, below_factor_1, selector_1, pivot_inverse_2, below_factor_2, selector_2, pivot_inverse_3, below_factor_3, selector_3):
    sigma_diag_0 = product(pivot_inverse_0.T, pivot_inverse_0)
    fronts = sigma_diag_0[None]
    sigma_diag_1, sigma_below_1, fronts = sweep_level(fronts, selector_1, pivot_inverse_1, below_factor_1, U1, True)
    sigma_diag_2, sigma_below_2, fronts = sweep_level(fronts, selector_2, pivot_inverse_2, below_factor_2, U2, True)
    sigma_diag_3, sigma_below_3, unused = sweep_level(fronts, selector_3, pivot_inverse_3, below_factor_3, U3, False)
    return (sigma_diag_0, sigma_diag_1, sigma_below_1, sigma_diag_2, sigma_below_2, sigma_diag_3, sigma_below_3)
```

```python
import jax
import jax.numpy as jnp
from jax import lax
from jax.sharding import Mesh, PartitionSpec as P

S = 1024
BLOCK = 128
U1 = 512
U2 = 1024
U3 = 1536
COLS = 256
PRECISION = lax.Precision.HIGH


def product(left, right):
    return jnp.dot(left, right, precision=PRECISION, preferred_element_type=jnp.float32)


def inner_product(left, right):
    return lax.dot_general(
        left,
        right,
        (((0,), (0,)), ((), ())),
        precision=PRECISION,
        preferred_element_type=jnp.float32,
    )


def swapped(array, axis, distance):
    return lax.ppermute(array, axis, [(i, i ^ distance) for i in range(lax.axis_size(axis))])


def gathered(values, axes, parts):
    spread = jnp.broadcast_to(values[None], (parts,) + values.shape)
    return lax.all_to_all(spread, axes, 0, 0)


def paired(values, axis, stack_axis):
    other = swapped(values, axis, 1)
    second = lax.axis_index(axis) == 1
    return jnp.where(
        second, jnp.stack([other, values], stack_axis), jnp.stack([values, other], stack_axis)
    )


def wide(pieces):
    return jnp.concatenate([pieces[part] for part in range(pieces.shape[0])], 1)


def gathered_x(values):
    me = lax.axis_index("x")
    rows = values.shape[0]
    out = jnp.zeros((rows, 4 * COLS), values.dtype)
    for distance in (0, 1, 3, 2):
        piece = swapped(values, "x", distance) if distance else values
        out = lax.dynamic_update_slice(out, piece, (0, (me ^ distance) * COLS))
    return out


def group_rows(values):
    return paired(gathered(values, "y", 4), "c", 1)


def group_sums(partial):
    core = lax.axis_index("c")
    keeping = lax.dynamic_index_in_dim(partial, core, 1, keepdims=False)
    sending = lax.dynamic_index_in_dim(partial, 1 - core, 1, keepdims=False)
    half = keeping + swapped(sending, "c", 1)
    return jnp.sum(lax.all_to_all(half, "y", 0, 0), 0)


def chosen(rows, selector, count):
    return jnp.concatenate(
        [
            lax.dynamic_slice_in_dim(rows, selector[block] * BLOCK, BLOCK, 1)
            for block in range(count)
        ],
        1,
    )


def columns(rows, start, length):
    return lax.dynamic_slice_in_dim(rows, start, length, 1)


def split(rows):
    return rows.reshape(4, 2, rows.shape[0] // 8, COLS)


def shards(v0, v1, b1, selector_1, v2, b2, selector_2, v3, b3, selector_3):
    half = lax.axis_index("h")
    quarter = lax.axis_index("q")
    pair = lax.axis_index("p")
    front_1 = half
    front_2 = half * 2 + quarter
    front_3 = front_2 * 2 + pair
    slot_1 = quarter * 2 + pair
    mine_1 = lax.dynamic_index_in_dim(selector_1, front_1, 0, keepdims=False)
    mine_2 = lax.dynamic_index_in_dim(selector_2, front_2, 0, keepdims=False)
    mine_3 = lax.dynamic_index_in_dim(selector_3, front_3, 0, keepdims=False)

    level_2 = paired(jnp.concatenate([v2, b2], 0), "p", 0)
    level_1 = gathered(jnp.concatenate([v1, b1], 0), ("q", "p"), 4)
    level_0 = gathered(v0, ("h", "q", "p"), 8)
    v0 = level_0.reshape(128, COLS)
    v1 = level_1[:, :32].reshape(128, COLS)
    b1 = level_1[:, 32:].reshape(64, COLS)
    v2 = level_2[:, :64].reshape(128, COLS)
    b2 = level_2[:, 64:].reshape(128, COLS)

    factor_rows = gathered_x(jnp.concatenate([b1, b2, b3], 0))
    inverse_columns = group_rows(jnp.concatenate([v1, v2, v3], 0))
    v1_columns = (
        inverse_columns[:, :, :128].reshape(8, 4, 32, COLS).swapaxes(0, 1).reshape(S, COLS)
    )
    v2_columns = (
        inverse_columns[:, :, 128:256].reshape(8, 2, 64, COLS).swapaxes(0, 1).reshape(S, COLS)
    )
    v3_columns = inverse_columns[:, :, 256:].reshape(S, COLS)
    w1 = product(factor_rows[:64], v1_columns)
    w2 = product(factor_rows[64:192], v2_columns)
    w3 = product(factor_rows[192:], v3_columns)
    inverse_rows = gathered_x(jnp.concatenate([v0, v1, v2, v3], 0))
    coupling_columns = group_rows(jnp.concatenate([w1, w2, w3], 0))
    w1_columns = (
        coupling_columns[:, :, :64].reshape(8, 4, 16, COLS).swapaxes(0, 1).reshape(U1, COLS)
    )
    w2_columns = (
        coupling_columns[:, :, 64:192].reshape(8, 2, 64, COLS).swapaxes(0, 1).reshape(U2, COLS)
    )
    w3_columns = coupling_columns[:, :, 192:].reshape(U3, COLS)
    w3_rows = gathered_x(w3)

    v0_rows = inverse_rows[:128]
    v1_rows = inverse_rows[128:256]
    v2_rows = inverse_rows[256:384]
    v3_rows = inverse_rows[384:]
    f0 = chosen(v0_rows, mine_1, 4)
    m1 = product(f0, w1_columns)
    m1_rows = gathered_x(m1)
    x1 = jnp.concatenate(
        [
            jnp.concatenate([v1_rows, jnp.zeros((128, U1), jnp.float32)], 1),
            jnp.concatenate([-m1_rows, f0], 1),
        ],
        0,
    )
    f1 = chosen(x1, mine_2, 8)
    m2 = product(f1, w2_columns)
    m2_rows = gathered_x(m2)
    x2 = jnp.concatenate(
        [
            jnp.concatenate([v2_rows, jnp.zeros((128, U2), jnp.float32)], 1),
            jnp.concatenate([-m2_rows, f1], 1),
        ],
        0,
    )
    f2 = chosen(x2, mine_3, 12)
    m3 = product(f2, w3_columns)

    d0 = inner_product(columns(v0_rows, front_3 * 128, 128), v0)
    d1 = inner_product(
        columns(x1, slot_1 * 256, 256), jnp.concatenate([v1, -m1], 0)
    )
    e1 = -inner_product(columns(f0, slot_1 * 128, 128), m1)
    d2 = inner_product(columns(x2, pair * 512, 512), jnp.concatenate([v2, -m2], 0))
    e2 = -inner_product(columns(f1, pair * 512, 512), m2)
    e3 = -inner_product(f2, m3)
    summed = group_sums(
        jnp.concatenate([split(d0), split(d1), split(e1), split(d2), split(e2), split(e3)], 2)
    )
    d0 = summed[:16]
    d1 = summed[16:48]
    e1 = summed[48:64]
    d2 = summed[64:128]
    e2 = summed[128:192]
    e3 = summed[192:]
    d3 = group_sums(split(inner_product(v3_rows, v3) - inner_product(w3_rows, e3)))
    return d0, d1, e1, d2, e2, d3, e3


def solution(mesh):
    devices = mesh.devices.reshape(2, 2, 2, 4, 2, 4)
    fine = Mesh(devices, ("h", "q", "p", "y", "c", "x"))
    tiled = P(("h", "q", "p", "y", "c"), "x")
    return jax.shard_map(
        shards,
        mesh=fine,
        in_specs=(tiled, tiled, tiled, P(), tiled, tiled, P(), tiled, tiled, P()),
        out_specs=(tiled,) * 7,
        check_vma=False,
    )
```

```python
import jax
import jax.numpy as jnp
from jax import lax
from jax.sharding import Mesh, PartitionSpec as P

S = 1024
BLOCK = 128
U1 = 512
U2 = 1024
U3 = 1536
COLS = 256
PRECISION = lax.Precision.HIGH


def product(left, right):
    return jnp.dot(left, right, precision=PRECISION, preferred_element_type=jnp.float32)


def inner_product(left, right):
    return lax.dot_general(
        left,
        right,
        (((0,), (0,)), ((), ())),
        precision=PRECISION,
        preferred_element_type=jnp.float32,
    )


def swapped(array, axis, distance):
    return lax.ppermute(array, axis, [(i, i ^ distance) for i in range(lax.axis_size(axis))])


def gathered(values, axes, parts):
    spread = jnp.broadcast_to(values[None], (parts,) + values.shape)
    return lax.all_to_all(spread, axes, 0, 0)


def paired(values, axis, stack_axis):
    other = swapped(values, axis, 1)
    second = lax.axis_index(axis) == 1
    return jnp.where(
        second, jnp.stack([other, values], stack_axis), jnp.stack([values, other], stack_axis)
    )


def wide(pieces):
    return jnp.concatenate([pieces[part] for part in range(pieces.shape[0])], 1)


def gathered_x(values):
    me = lax.axis_index("x")
    rows = values.shape[0]
    out = jnp.zeros((rows, 4 * COLS), values.dtype)
    for distance in (0, 1, 3, 2):
        piece = swapped(values, "x", distance) if distance else values
        out = lax.dynamic_update_slice(out, piece, (0, (me ^ distance) * COLS))
    return out


def group_rows(values):
    return paired(gathered(values, "y", 4), "c", 1)


def group_sums(partial):
    core = lax.axis_index("c")
    keeping = lax.dynamic_index_in_dim(partial, core, 1, keepdims=False)
    sending = lax.dynamic_index_in_dim(partial, 1 - core, 1, keepdims=False)
    half = keeping + swapped(sending, "c", 1)
    return jnp.sum(lax.all_to_all(half, "y", 0, 0), 0)


def chosen(rows, selector, count):
    return jnp.concatenate(
        [
            lax.dynamic_slice_in_dim(rows, selector[block] * BLOCK, BLOCK, 1)
            for block in range(count)
        ],
        1,
    )


def columns(rows, start, length):
    return lax.dynamic_slice_in_dim(rows, start, length, 1)


def split(rows):
    return rows.reshape(4, 2, rows.shape[0] // 8, COLS)


def shards(v0, v1, b1, selector_1, v2, b2, selector_2, v3, b3, selector_3):
    half = lax.axis_index("h")
    quarter = lax.axis_index("q")
    pair = lax.axis_index("p")
    front_1 = half
    front_2 = half * 2 + quarter
    front_3 = front_2 * 2 + pair
    slot_1 = quarter * 2 + pair
    mine_1 = lax.dynamic_index_in_dim(selector_1, front_1, 0, keepdims=False)
    mine_2 = lax.dynamic_index_in_dim(selector_2, front_2, 0, keepdims=False)
    mine_3 = lax.dynamic_index_in_dim(selector_3, front_3, 0, keepdims=False)

    level_2 = paired(jnp.concatenate([v2, b2], 0), "p", 0)
    level_1 = paired(jnp.concatenate([v1, b1, v0], 0), "p", 0)
    level_1 = paired(level_1, "q", 0).reshape(4, 64, COLS)
    v0 = level_1[:, 48:].reshape(64, COLS)
    v0 = jnp.concatenate([v0, swapped(v0, "h", 1)], 0)
    v1 = level_1[:, :32].reshape(128, COLS)
    b1 = level_1[:, 32:48].reshape(64, COLS)
    v2 = level_2[:, :64].reshape(128, COLS)
    b2 = level_2[:, 64:].reshape(128, COLS)

    b3_rows = gathered_x(b3)
    v3_columns = group_rows(v3).reshape(S, COLS)

    b2_rows = gathered_x(b2)
    early, v3_columns = lax.optimization_barrier(
        (jnp.concatenate([v1, v2, b1], 0), v3_columns)
    )
    w3 = product(b3_rows, v3_columns)
    early = group_rows(early)
    v1_columns = early[:, :, :128].reshape(8, 4, 32, COLS).swapaxes(0, 1).reshape(S, COLS)
    v2_columns = early[:, :, 128:256].reshape(8, 2, 64, COLS).swapaxes(0, 1).reshape(S, COLS)
    b1_columns = early[:, :, 256:].reshape(8, 4, 16, COLS).swapaxes(0, 1).reshape(U1, COLS)
    w2 = product(b2_rows, v2_columns)
    w2_part = gathered(w2, "y", 4)

    v0_rows = gathered_x(v0)
    f0 = chosen(v0_rows, mine_1, 4)
    y1_rows, w2_part, w3 = lax.optimization_barrier(
        (gathered_x(product(f0, b1_columns)), w2_part, w3)
    )
    w2_columns = (
        paired(w2_part, "c", 1).reshape(8, 2, 64, COLS).swapaxes(0, 1).reshape(U2, COLS)
    )
    m1 = product(y1_rows, v1_columns)
    m1_rows = gathered_x(m1)
    ancestor_rows = gathered_x(jnp.concatenate([v1, v2], 0))
    v1_rows = ancestor_rows[:128]
    v2_rows = ancestor_rows[128:]
    x1 = jnp.concatenate(
        [
            jnp.concatenate([v1_rows, jnp.zeros((128, U1), jnp.float32)], 1),
            jnp.concatenate([-m1_rows, f0], 1),
        ],
        0,
    )
    f1 = chosen(x1, mine_2, 8)
    m2 = product(f1, w2_columns)
    m2_rows = gathered_x(m2)
    w3_columns = group_rows(w3).reshape(U3, COLS)

    d0 = inner_product(columns(v0_rows, front_3 * 128, 128), v0)
    d1 = inner_product(columns(x1, slot_1 * 256, 256), jnp.concatenate([v1, -m1], 0))
    e1 = -inner_product(columns(f0, slot_1 * 128, 128), m1)
    e2 = -inner_product(columns(f1, pair * 512, 512), m2)
    summed = group_sums(jnp.concatenate([split(d0), split(d1), split(e1), split(e2)], 2))

    m2_rows, w3_columns, summed = lax.optimization_barrier((m2_rows, w3_columns, summed))
    d0 = summed[:16]
    d1 = summed[16:48]
    e1 = summed[48:64]
    e2 = summed[64:]
    x2 = jnp.concatenate(
        [
            jnp.concatenate([v2_rows, jnp.zeros((128, U2), jnp.float32)], 1),
            jnp.concatenate([-m2_rows, f1], 1),
        ],
        0,
    )
    f2 = chosen(x2, mine_3, 12)
    m3 = product(f2, w3_columns)
    own_rows, m3 = lax.optimization_barrier((jnp.concatenate([v3, w3], 0), m3))
    own_rows = gathered_x(own_rows)
    v3_rows = own_rows[:128]
    w3_rows = own_rows[128:]
    d2 = inner_product(columns(x2, pair * 512, 512), jnp.concatenate([v2, -m2], 0))
    e3 = -inner_product(f2, m3)
    summed = group_sums(jnp.concatenate([split(d2), split(e3)], 2))
    d2 = summed[:64]
    e3 = summed[64:]
    d3 = group_sums(split(inner_product(v3_rows, v3) - inner_product(w3_rows, e3)))
    return d0, d1, e1, d2, e2, d3, e3


def solution(mesh):
    devices = mesh.devices.reshape(2, 2, 2, 4, 2, 4)
    fine = Mesh(devices, ("h", "q", "p", "y", "c", "x"))
    tiled = P(("h", "q", "p", "y", "c"), "x")
    return jax.shard_map(
        shards,
        mesh=fine,
        in_specs=(tiled, tiled, tiled, P(), tiled, tiled, P(), tiled, tiled, P()),
        out_specs=(tiled,) * 7,
        check_vma=False,
    )
```

```python
import jax
import jax.numpy as jnp
from jax import lax
from jax.experimental import pallas as pl
from jax.experimental.pallas import tpu as pltpu
from jax.sharding import Mesh, PartitionSpec as P

S = 1024
BLOCK = 128
U1 = 512
U2 = 1024
U3 = 1536
COLS = 256
F32 = jnp.float32

CORE, PART, SLOT, PAIR, FRONT, SEL1, SEL2, SEL3 = 0, 1, 2, 3, 4, 8, 12, 20


def halves(values):
    high = values.astype(jnp.bfloat16)
    return high, (values - high.astype(F32)).astype(jnp.bfloat16)


def dot(left, right, contract=((1,), (0,))):
    left_high, left_low = halves(left)
    right_high, right_low = halves(right)

    def one(a, b):
        return lax.dot_general(a, b, (contract, ((), ())), preferred_element_type=F32)

    return one(left_high, right_high) + (one(left_high, right_low) + one(left_low, right_high))


def inner(left, right):
    return dot(left, right, ((0,), (0,)))


def times(number, unit):
    return pl.multiple_of(number * unit, unit)


def ordered(core, own, other):
    return [jnp.where(core == 0, own, other), jnp.where(core == 0, other, own)]


def call(body, micros, outs, scratch, *operands):
    spec = pl.BlockSpec(memory_space=pltpu.VMEM)
    return pl.pallas_call(
        body,
        out_shape=[jax.ShapeDtypeStruct(shape, F32) for shape in outs],
        in_specs=[pl.BlockSpec(memory_space=pltpu.SMEM)] + [spec] * (len(operands) - 1),
        out_specs=[spec] * len(outs),
        scratch_shapes=[pltpu.VMEM(shape, F32) for shape in scratch],
        cost_estimate=pl.CostEstimate(
            flops=micros * 1_100_000_000, bytes_accessed=0, transcendentals=0
        ),
        compiler_params=pltpu.CompilerParams(vmem_limit_bytes=24 * 1024 * 1024),
    )(*operands)


def place_ancestors(ids, own_1, pair_1, quad_1, own_2, pair_2, early, row_2, row_1, row_0):
    slot, pair = ids[SLOT], ids[PAIR]
    level_1 = [own_1[...], pair_1[...], quad_1[0:64, :], quad_1[64:128, :]]
    for distance in range(4):
        source = slot ^ distance
        values = level_1[distance]
        row_1[pl.ds(times(source, 32), 32), :] = values[0:32]
        row_0[pl.ds(times(source, 16), 16), :] = values[48:64]
        for copy in range(4):
            early[copy, pl.ds(times(source, 32), 32), :] = values[0:32]
            early[copy, pl.ds(256 + times(source, 16), 16), :] = values[32:48]
    for distance, ref in enumerate((own_2, pair_2)):
        start = times(pair ^ distance, 64)
        values = ref[...]
        row_2[pl.ds(start, 64), :] = values[64:128]
        row_2[pl.ds(128 + start, 64), :] = values[0:64]
        for copy in range(4):
            early[copy, pl.ds(128 + start, 64), :] = values[0:64]


def couple(ids, a0, a1, a2, a3, b0, b1, b2, b3, own_3, other_3, own, other, out):
    core, part = ids[CORE], ids[PART]
    w2 = jnp.zeros((128, COLS), F32)
    w3 = jnp.zeros((192, COLS), F32)
    for distance, (left_3, left_2) in enumerate(zip((a0, a1, a2, a3), (b0, b1, b2, b3))):
        quarter = part ^ distance
        w3 += dot(
            left_3[0:192, :], jnp.concatenate(ordered(core, own_3[quarter], other_3[quarter]), 0)
        )
        rows = []
        for step in range(2):
            y = (quarter & 1) * 2 + step
            start = 128 + times(quarter >> 1, 64)
            rows += ordered(core, own[y, pl.ds(start, 64), :], other[y, pl.ds(start, 64), :])
        w2 += dot(left_2[0:128, :], jnp.concatenate(rows, 0))
    for copy in range(4):
        out[copy, 0:128, :] = w2
        out[copy, 128:320, :] = w3


def first_half(ids, c0, c1, c2, c3, own, other, f0, y1, rows_0):
    core, part = ids[CORE], ids[PART]
    for distance, ref in enumerate((c0, c1, c2, c3)):
        rows_0[:, pl.ds(times(part ^ distance, COLS), COLS)] = ref[128:256, :]
    for block in range(4):
        f0[:, block * BLOCK : (block + 1) * BLOCK] = rows_0[
            :, pl.ds(times(ids[SEL1 + block], BLOCK), BLOCK)
        ]
    rows = []
    for slot in range(4):
        start = 256 + slot * 16
        for y in range(4):
            rows += ordered(core, own[y, start : start + 16, :], other[y, start : start + 16, :])
    y1[...] = dot(f0[...], jnp.concatenate(rows, 0))


def second_half(ids, y0, y1, y2, y3, own, other, m1):
    core, part = ids[CORE], ids[PART]
    total = jnp.zeros((128, COLS), F32)
    for distance, ref in enumerate((y0, y1, y2, y3)):
        start = times(part ^ distance, 32)
        rows = []
        for y in range(4):
            rows += ordered(core, own[y, pl.ds(start, 32), :], other[y, pl.ds(start, 32), :])
        total += dot(ref[...], jnp.concatenate(rows, 0))
    m1[...] = total


def level_two(ids, c0, c1, c2, c3, m0, m1, m2, m3, f0, own, other, x1, f1, out):
    core, part = ids[CORE], ids[PART]
    x1[0:128, S:] = jnp.zeros((128, U1), F32)
    x1[128:256, S:] = f0[...]
    for distance, (v_ref, m_ref) in enumerate(zip((c0, c1, c2, c3), (m0, m1, m2, m3))):
        place = pl.ds(times(part ^ distance, COLS), COLS)
        x1[0:128, place] = v_ref[0:128, :]
        x1[128:256, place] = -m_ref[...]
    for block in range(8):
        f1[:, block * BLOCK : (block + 1) * BLOCK] = x1[
            :, pl.ds(times(ids[SEL2 + block], BLOCK), BLOCK)
        ]
    total = jnp.zeros((256, COLS), F32)
    for pair in range(2):
        rows = []
        for y in range(4):
            start = pair * 64
            rows += ordered(core, own[y, start : start + 64, :], other[y, start : start + 64, :])
        total += dot(f1[:, pair * 512 : (pair + 1) * 512], jnp.concatenate(rows, 0))
    out[...] = total


def put(core, keep, send, values, start, rows):
    for y in range(4):
        first = values[2 * y * rows : (2 * y + 1) * rows]
        second = values[(2 * y + 1) * rows : (2 * y + 2) * rows]
        keep[y, start : start + rows, :] = jnp.where(core == 0, first, second)
        send[y, start : start + rows, :] = jnp.where(core == 0, second, first)


def early_sums(ids, c0, c1, c2, c3, f0, m1, x1, f1, m2, keep, send, piece):
    core, part = ids[CORE], ids[PART]
    front, slot, pair = ids[FRONT], ids[SLOT], ids[PAIR]
    for distance, ref in enumerate((c0, c1, c2, c3)):

        @pl.when((part ^ distance) == front >> 1)
        def _():
            piece[...] = ref[128:256, pl.ds(times(front & 1, BLOCK), BLOCK)]

    v = c0[...]
    put(core, keep, send, inner(piece[...], v[128:256]), 0, 16)
    m = m1[...]
    d1 = inner(x1[:, pl.ds(times(slot, 256), 256)], jnp.concatenate([v[0:128], -m], 0))
    put(core, keep, send, d1, 16, 32)
    put(core, keep, send, inner(f0[:, pl.ds(times(slot, 128), 128)], -m), 48, 16)
    put(core, keep, send, inner(f1[:, pl.ds(times(pair, 512), 512)], -m2[...]), 64, 64)


def level_three(ids, b0, b1, b2, b3, m0, m1, m2, m3, f1, own, other, keep_1, send_1, keep, send, x2, f2):
    core, part, pair = ids[CORE], ids[PART], ids[PAIR]
    x2[0:128, S:] = jnp.zeros((128, U2), F32)
    x2[128:384, S:] = f1[...]
    for distance, (v_ref, m_ref) in enumerate(zip((b0, b1, b2, b3), (m0, m1, m2, m3))):
        place = pl.ds(times(part ^ distance, COLS), COLS)
        x2[0:128, place] = v_ref[128:256, :]
        x2[128:384, place] = -m_ref[...]
    for block in range(12):
        f2[:, block * BLOCK : (block + 1) * BLOCK] = x2[
            :, pl.ds(times(ids[SEL3 + block], BLOCK), BLOCK)
        ]
    total = jnp.zeros((384, COLS), F32)
    for y in range(4):
        rows = jnp.concatenate(ordered(core, own[y, 128:320, :], other[y, 128:320, :]), 0)
        total += dot(f2[:, y * 384 : (y + 1) * 384], rows)
    for y in range(4):
        keep[y, 0:128, :] = keep_1[y]
        send[y, 0:128, :] = send_1[y]
    put(core, keep, send, inner(f2[...], -total), 192, 192)
    mine = jnp.concatenate([b0[128:256, :], -m0[...]], 0)
    put(core, keep, send, inner(x2[:, pl.ds(times(pair, 512), 512)], mine), 128, 64)


def last_level(ids, parts, a0, a1, a2, a3, w0, w1, w2, w3, early, d2, e3, keep, send):
    core, part = ids[CORE], ids[PART]
    total = (parts[0] + parts[1]) + (parts[2] + parts[3])
    early[...] = total[0:128]
    d2[...] = total[128:192]
    below = total[192:384]
    e3[...] = below
    right = jnp.concatenate([a0[192:320, :], -below], 0)
    for distance, (v_ref, w_ref) in enumerate(zip((a0, a1, a2, a3), (w0, w1, w2, w3))):
        rows = inner(jnp.concatenate([v_ref[192:320, :], w_ref[...]], 0), right)
        place = part ^ distance
        keep[place] = jnp.where(core == 0, rows[0:128], rows[128:256])
        send[place] = jnp.where(core == 0, rows[128:256], rows[0:128])


def swapped(array, axis, distance):
    return lax.ppermute(array, axis, [(i, i ^ distance) for i in range(lax.axis_size(axis))])


def around(values):
    return [values] + [swapped(values, "x", distance) for distance in (1, 2, 3)]


def exchanged(values):
    return lax.all_to_all(values, "y", 0, 0)


def spread(values):
    return jnp.broadcast_to(values[None], (4,) + values.shape)


def shards(v0, v1, b1, selector_1, v2, b2, selector_2, v3, b3, selector_3):
    half = lax.axis_index("h")
    quarter = lax.axis_index("q")
    pair = lax.axis_index("p")
    front_2 = half * 2 + quarter
    front_3 = front_2 * 2 + pair
    slot = quarter * 2 + pair
    places = jnp.stack(
        [lax.axis_index("c"), lax.axis_index("x"), slot, pair, front_3] + [jnp.int32(0)] * 3
    ).astype(jnp.int32)
    ids = jnp.concatenate(
        [
            places,
            lax.dynamic_index_in_dim(selector_1, half, 0, keepdims=False),
            lax.dynamic_index_in_dim(selector_2, front_2, 0, keepdims=False),
            lax.dynamic_index_in_dim(selector_3, front_3, 0, keepdims=False),
        ]
    )

    own_rows = around(jnp.concatenate([b3, v3], 0))
    own_1 = jnp.concatenate([v1, b1, v0], 0)
    pair_1 = swapped(own_1, "p", 1)
    own_2 = jnp.concatenate([v2, b2], 0)
    pair_2 = swapped(own_2, "p", 1)
    quad_1 = swapped(jnp.concatenate([own_1, pair_1], 0), "q", 1)
    columns_3 = exchanged(spread(v3))
    early, row_2, row_1, row_0 = call(
        place_ancestors,
        2,
        [(4, 320, COLS), (256, COLS), (128, COLS), (64, COLS)],
        [],
        ids, own_1, pair_1, quad_1, own_2, pair_2,
    )
    early, columns_3, own_rows = lax.optimization_barrier((early, columns_3, own_rows))
    other_3 = swapped(columns_3, "c", 1)
    early = exchanged(early)
    rows_2 = around(row_2)
    rows_10 = around(jnp.concatenate([row_1, row_0, swapped(row_0, "h", 1)], 0))
    early, rows_2, rows_10 = lax.optimization_barrier((early, rows_2, rows_10))
    early_other = swapped(early, "c", 1)

    (coupling,) = call(
        couple, 4, [(4, 320, COLS)], [], ids, *own_rows, *rows_2, columns_3, other_3, early, early_other
    )
    f0, y1 = call(
        first_half, 2, [(128, U1), (128, COLS)], [(128, S)], ids, *rows_10, early, early_other
    )
    w3 = coupling[0, 128:320]
    coupling = exchanged(coupling)
    y1 = around(y1)
    (m1,) = call(second_half, 2, [(128, COLS)], [], ids, *y1, early, early_other)
    m1, coupling = lax.optimization_barrier((around(m1), coupling))
    coupling_other = swapped(coupling, "c", 1)
    x1, f1, m2 = call(
        level_two,
        3,
        [(256, S + U1), (256, U2), (256, COLS)],
        [],
        ids, *rows_10, *m1, f0, coupling, coupling_other,
    )
    keep, send = call(
        early_sums,
        3,
        [(4, 128, COLS), (4, 128, COLS)],
        [(128, BLOCK)],
        ids, *rows_10, f0, m1[0], x1, f1, m2,
    )
    m2 = around(m2)
    keep, send = call(
        level_three,
        6,
        [(4, 384, COLS), (4, 384, COLS)],
        [(384, S + U2), (384, U3)],
        ids, *rows_2, *m2, f1, coupling, coupling_other, keep, send,
    )
    w3, keep, send = lax.optimization_barrier((w3, keep, send))
    w3 = around(w3)
    summed, d2, e3, keep, send = call(
        last_level,
        3,
        [(128, COLS), (64, COLS), (192, COLS), (4, 128, COLS), (4, 128, COLS)],
        [],
        ids, exchanged(keep + swapped(send, "c", 1)), *own_rows, *w3,
    )
    d3 = jnp.sum(exchanged(keep + swapped(send, "c", 1)), 0)
    return summed[:16], summed[16:48], summed[48:64], d2, summed[64:], d3, e3


def solution(mesh):
    devices = mesh.devices.reshape(2, 2, 2, 4, 2, 4)
    fine = Mesh(devices, ("h", "q", "p", "y", "c", "x"))
    tiled = P(("h", "q", "p", "y", "c"), "x")
    return jax.shard_map(
        shards,
        mesh=fine,
        in_specs=(tiled, tiled, tiled, P(), tiled, tiled, P(), tiled, tiled, P()),
        out_specs=(tiled,) * 7,
        check_vma=False,
    )
```

```python
import jax
import jax.numpy as jnp
from jax import lax
from jax.experimental import pallas as pl
from jax.experimental.pallas import tpu as pltpu
from jax.sharding import Mesh, PartitionSpec as P

S = 1024
BLOCK = 128
U1 = 512
U2 = 1024
U3 = 1536
COLS = 256
F32 = jnp.float32

CORE, PART, SLOT, PAIR, FRONT = 0, 1, 2, 3, 4


def halves(values):
    high = values.astype(jnp.bfloat16)
    return high, (values - high.astype(F32)).astype(jnp.bfloat16)


def dot(left, right, contract=((1,), (0,))):
    left_high, left_low = halves(left)
    right_high, right_low = halves(right)

    def one(a, b):
        return lax.dot_general(a, b, (contract, ((), ())), preferred_element_type=F32)

    return one(left_high, right_high) + (one(left_high, right_low) + one(left_low, right_high))


def inner(left, right):
    return dot(left, right, ((0,), (0,)))


def times(number, unit):
    return pl.multiple_of(number * unit, unit)


def ordered(core, own, other):
    return [jnp.where(core == 0, own, other), jnp.where(core == 0, other, own)]


class Far:

    def __init__(self, value, start=0, rows=None):
        self.value = value
        self.start = start
        self.shape = value if isinstance(value, tuple) else value.shape
        self.shape = (rows or self.shape[0],) + tuple(self.shape[1:])


def call(body, micros, outs, scratch, *operands):
    away_in = [at for at, operand in enumerate(operands) if isinstance(operand, Far)]
    away_out = [at for at, out in enumerate(outs) if isinstance(out, Far)]
    values = [operand.value if isinstance(operand, Far) else operand for operand in operands]
    shapes = [out.value if isinstance(out, Far) else out for out in outs]
    fetched = [operands[at].shape for at in away_in]
    returned = [shapes[at] for at in away_out]
    near = pl.BlockSpec(memory_space=pltpu.VMEM)
    distant = pl.BlockSpec(memory_space=pltpu.HBM)

    def place(at, value):
        if at in away_in:
            return distant
        return near if value.dtype == F32 else pl.BlockSpec(memory_space=pltpu.SMEM)

    def kernel(*refs):
        inputs = list(refs[: len(values)])
        results = list(refs[len(values) : len(values) + len(outs)])
        own = list(refs[len(values) + len(outs) :])
        held = own[: len(scratch)]
        buffers = own[len(scratch) :]
        copies = []
        for number, at in enumerate(away_in):
            rows = pl.ds(operands[at].start, fetched[number][0])
            copy = pltpu.make_async_copy(
                inputs[at].at[rows], buffers[number], buffers[-1].at[number]
            )
            copy.start()
            copies.append(copy)
            inputs[at] = buffers[number]
        for copy in copies:
            copy.wait()
        copies = []
        for number, at in enumerate(away_out):
            number += len(away_in)
            copies.append(
                pltpu.make_async_copy(buffers[number], results[at], buffers[-1].at[number])
            )
            results[at] = buffers[number]
        body(*inputs, *results, *held)
        for copy in copies:
            copy.start()
        for copy in copies:
            copy.wait()

    count = len(fetched) + len(returned)
    return pl.pallas_call(
        kernel,
        out_shape=[jax.ShapeDtypeStruct(shape, F32) for shape in shapes],
        in_specs=[place(at, value) for at, value in enumerate(values)],
        out_specs=[distant if at in away_out else near for at in range(len(outs))],
        scratch_shapes=[pltpu.VMEM(shape, F32) for shape in scratch + fetched + returned]
        + ([pltpu.SemaphoreType.DMA((count,))] if count else []),
        cost_estimate=pl.CostEstimate(
            flops=micros * 1_100_000_000, bytes_accessed=0, transcendentals=0
        ),
        compiler_params=pltpu.CompilerParams(vmem_limit_bytes=28 * 1024 * 1024),
    )(*values)


def pack(v0, v1, b1, v2, b2, v3, b3, own_1, own_2, own_3, columns_3):
    own_1[0:32, :] = v1[...]
    own_1[32:48, :] = b1[...]
    own_1[48:64, :] = v0[...]
    own_2[0:64, :] = v2[...]
    own_2[64:128, :] = b2[...]
    own_3[0:192, :] = b3[...]
    own_3[192:320, :] = v3[...]
    for copy in range(4):
        columns_3[copy] = v3[...]


def place_ancestors(ids, p0, p1, p2, p3, own_2, pair_2, early, rows, row_0):
    slot, pair = ids[SLOT], ids[PAIR]
    for distance, ref in enumerate((p0, p1, p2, p3)):
        source = slot ^ distance
        values = ref[...]
        rows[pl.ds(256 + times(source, 32), 32), :] = values[0:32]
        rows[pl.ds(384 + times(source, 16), 16), :] = values[48:64]
        row_0[pl.ds(times(source, 16), 16), :] = values[48:64]
        for copy in range(4):
            early[copy, pl.ds(times(source, 32), 32), :] = values[0:32]
            early[copy, pl.ds(256 + times(source, 16), 16), :] = values[32:48]
    for distance, ref in enumerate((own_2, pair_2)):
        start = times(pair ^ distance, 64)
        values = ref[...]
        rows[pl.ds(start, 64), :] = values[64:128]
        rows[pl.ds(128 + start, 64), :] = values[0:64]
        for copy in range(4):
            early[copy, pl.ds(128 + start, 64), :] = values[0:64]


def add(left, right, out):
    out[...] = left[...] + right[...]


def add_four(parts, out):
    out[...] = (parts[0] + parts[1]) + (parts[2] + parts[3])


def couple_front(ids, a0, a1, a2, a3, own, other, w3, v3):
    core, part = ids[CORE], ids[PART]
    total = jnp.zeros((192, COLS), F32)
    for distance, ref in enumerate((a0, a1, a2, a3)):
        quarter = part ^ distance
        total += dot(ref[0:192, :], jnp.concatenate(ordered(core, own[quarter], other[quarter]), 0))
        v3[:, pl.ds(times(quarter, COLS), COLS)] = ref[192:320, :]
    w3[...] = total


def shelve(ids, r0, r1, r2, r3, held):
    for distance, ref in enumerate((r0, r1, r2, r3)):
        held[:, pl.ds(times(ids[PART] ^ distance, COLS), COLS)] = ref[...]


def middle(
    ids, sel, b2, v0_top, h0, h1, h2, h3, own, other, w3, coupling, y1, f0, v0, v1_columns
):
    core, part = ids[CORE], ids[PART]
    v0[0:64, :] = v0_top[...]
    for distance, ref in enumerate((h0, h1, h2, h3)):
        v0[64:128, pl.ds(times(part ^ distance, COLS), COLS)] = ref[...]
    for block in range(4):
        f0[:, block * BLOCK : (block + 1) * BLOCK] = v0[
            :, pl.ds(times(sel[ids[FRONT] >> 2, block], BLOCK), BLOCK)
        ]
    rows = []
    for slot in range(4):
        start = 256 + slot * 16
        for y in range(4):
            rows += ordered(core, own[y, start : start + 16, :], other[y, start : start + 16, :])
    y1[...] = dot(f0[...], jnp.concatenate(rows, 0))
    w2 = jnp.zeros((128, COLS), F32)
    for pair in range(2):
        rows = []
        start = 128 + pair * 64
        for y in range(4):
            rows += ordered(core, own[y, start : start + 64, :], other[y, start : start + 64, :])
        w2 += dot(b2[:, pair * 512 : (pair + 1) * 512], jnp.concatenate(rows, 0))
    for copy in range(4):
        coupling[copy, 0:128, :] = w2
        coupling[copy, 128:320, :] = w3[...]
    for slot in range(4):
        start = slot * 32
        for y in range(4):
            place = slot * 256 + y * 64
            first, second = ordered(
                core, own[y, start : start + 32, :], other[y, start : start + 32, :]
            )
            v1_columns[place : place + 32, :] = first
            v1_columns[place + 32 : place + 64, :] = second


def second_half(ids, y0, y1, y2, y3, v1_columns, m1):
    part = ids[PART]
    total = jnp.zeros((128, COLS), F32)
    for distance, ref in enumerate((y0, y1, y2, y3)):
        total += dot(ref[...], v1_columns[pl.ds(times(part ^ distance, COLS), COLS), :])
    m1[...] = total


def level_two(
    ids, sel, v1, f0, m0, m1, m2, m3, own, other, out, f1, w3_columns, x1_part, mine, x1
):
    core, part, slot = ids[CORE], ids[PART], ids[SLOT]
    x1[0:128, 0:S] = v1[...]
    x1[0:128, S:] = jnp.zeros((128, U1), F32)
    x1[128:256, S:] = f0[...]
    for distance, ref in enumerate((m0, m1, m2, m3)):
        x1[128:256, pl.ds(times(part ^ distance, COLS), COLS)] = -ref[...]
    for block in range(8):
        f1[:, block * BLOCK : (block + 1) * BLOCK] = x1[
            :, pl.ds(times(sel[ids[FRONT] >> 1, block], BLOCK), BLOCK)
        ]
    total = jnp.zeros((256, COLS), F32)
    for pair in range(2):
        rows = []
        for y in range(4):
            start = pair * 64
            rows += ordered(core, own[y, start : start + 64, :], other[y, start : start + 64, :])
        total += dot(f1[:, pair * 512 : (pair + 1) * 512], jnp.concatenate(rows, 0))
    out[...] = total
    for y in range(4):
        first, second = ordered(core, own[y, 128:320, :], other[y, 128:320, :])
        w3_columns[y * 384 : y * 384 + 192, :] = first
        w3_columns[y * 384 + 192 : y * 384 + 384, :] = second
    x1_part[...] = x1[:, pl.ds(times(slot, 256), 256)]
    mine[...] = x1[:, pl.ds(times(part, COLS), COLS)]


def put(core, keep, send, values, start, rows):
    for y in range(4):
        first = values[2 * y * rows : (2 * y + 1) * rows]
        second = values[(2 * y + 1) * rows : (2 * y + 2) * rows]
        keep[y, start : start + rows, :] = jnp.where(core == 0, first, second)
        send[y, start : start + rows, :] = jnp.where(core == 0, second, first)


def early_sums(ids, v0, f0, x1_part, mine, f1, m2, keep, send):
    core, part = ids[CORE], ids[PART]
    front, slot, pair = ids[FRONT], ids[SLOT], ids[PAIR]
    d0 = inner(v0[:, pl.ds(times(front, BLOCK), BLOCK)], v0[:, pl.ds(times(part, COLS), COLS)])
    put(core, keep, send, d0, 0, 16)
    put(core, keep, send, inner(x1_part[...], mine[...]), 16, 32)
    e1 = inner(f0[:, pl.ds(times(slot, BLOCK), BLOCK)], mine[128:256, :])
    put(core, keep, send, e1, 48, 16)
    put(core, keep, send, inner(f1[:, pl.ds(times(pair, 512), 512)], -m2[...]), 64, 64)


def level_three(
    ids, sel, v2, f1, w3_columns, keep_1, send_1, m0, m1, m2, m3, keep, send, x2, f2
):
    core, part, pair = ids[CORE], ids[PART], ids[PAIR]
    x2[0:128, 0:S] = v2[...]
    x2[0:128, S:] = jnp.zeros((128, U2), F32)
    x2[128:384, S:] = f1[...]
    for distance, ref in enumerate((m0, m1, m2, m3)):
        x2[128:384, pl.ds(times(part ^ distance, COLS), COLS)] = -ref[...]
    for block in range(12):
        f2[:, block * BLOCK : (block + 1) * BLOCK] = x2[
            :, pl.ds(times(sel[ids[FRONT], block], BLOCK), BLOCK)
        ]
    total = dot(f2[...], w3_columns[...])
    for y in range(4):
        keep[y, 0:128, :] = keep_1[y]
        send[y, 0:128, :] = send_1[y]
    put(core, keep, send, inner(f2[...], -total), 192, 192)
    mine = x2[:, pl.ds(times(part, COLS), COLS)]
    put(core, keep, send, inner(x2[:, pl.ds(times(pair, 512), 512)], mine), 128, 64)


def last_level(
    ids, parts, v3, w0, w1, w2, w3, d0, d1, e1, e2, d2, e3, keep, send
):
    core, part = ids[CORE], ids[PART]
    total = (parts[0] + parts[1]) + (parts[2] + parts[3])
    d0[...] = total[0:16]
    d1[...] = total[16:48]
    e1[...] = total[48:64]
    e2[...] = total[64:128]
    d2[...] = total[128:192]
    below = total[192:384]
    e3[...] = below
    right = jnp.concatenate([v3[:, pl.ds(times(part, COLS), COLS)], -below], 0)
    for distance, ref in enumerate((w0, w1, w2, w3)):
        place = part ^ distance
        left = jnp.concatenate([v3[:, pl.ds(times(place, COLS), COLS)], ref[...]], 0)
        rows = inner(left, right)
        keep[place] = jnp.where(core == 0, rows[0:128], rows[128:256])
        send[place] = jnp.where(core == 0, rows[128:256], rows[0:128])


def swapped(array, axis, distance, parts=2):
    return lax.ppermute(array, axis, [(i, i ^ distance) for i in range(parts)])


def around(values, axis="x"):
    return [values] + [swapped(values, axis, distance, 4) for distance in (1, 2, 3)]


def exchanged(values):
    return lax.all_to_all(values, "y", 0, 0)


def core_sum(keep, send):
    (total,) = call(add, 1, [keep.shape], [], keep, swapped(send, "c", 1))
    return exchanged(total)


def shards(v0, v1, b1, selector_1, v2, b2, selector_2, v3, b3, selector_3):
    half = lax.axis_index("h")
    quarter = lax.axis_index("q")
    pair = lax.axis_index("p")
    slot = quarter * 2 + pair
    ids = jnp.stack(
        [lax.axis_index("c"), lax.axis_index("x"), slot, pair, half * 4 + slot]
    ).astype(jnp.int32)

    own_1, own_2, own_3, columns_3 = call(
        pack,
        1,
        [(64, COLS), (128, COLS), (320, COLS), (4, 128, COLS)],
        [],
        *[Far(value) for value in (v0, v1, b1, v2, b2, v3, b3)],
    )
    ancestors = around(own_1, ("q", "p"))
    pair_2 = swapped(own_2, "p", 1)
    own_rows = around(own_3)
    columns_3 = exchanged(columns_3)
    early, rows, row_0 = call(
        place_ancestors,
        2,
        [(4, 320, COLS), (448, COLS), (64, COLS)],
        [],
        ids, *ancestors, own_2, pair_2,
    )
    early, columns_3 = lax.optimization_barrier((early, columns_3))
    early = exchanged(early)
    row_0 = around(swapped(row_0, "h", 1))
    w3, v3_rows = call(
        couple_front,
        2,
        [(192, COLS), Far((128, S))],
        [],
        ids, *own_rows, columns_3, swapped(columns_3, "c", 1),
    )
    (held,) = call(shelve, 1, [Far((448, S))], [], ids, *around(rows))
    early, row_0, w3, v3_rows, held = lax.optimization_barrier(
        (early, row_0, w3, v3_rows, held)
    )

    coupling, y1, f0, v0_rows, v1_columns = call(
        middle,
        4,
        [(4, 320, COLS), (128, COLS), Far((128, U1)), Far((128, S)), Far((S, COLS))],
        [],
        ids, selector_1, Far(held, 0, 128), Far(held, 384, 64), *row_0,
        early, swapped(early, "c", 1), w3,
    )
    coupling = exchanged(coupling)
    (m1,) = call(second_half, 2, [(128, COLS)], [], ids, *around(y1), Far(v1_columns))
    m1, coupling = lax.optimization_barrier((around(m1), coupling))
    m2, f1, w3_columns, x1_part, mine = call(
        level_two,
        3,
        [(256, COLS), Far((256, U2)), Far((U3, COLS)), Far((256, 256)), Far((256, COLS))],
        [(256, S + U1)],
        ids, selector_2, Far(held, 256, 128), Far(f0), *m1,
        coupling, swapped(coupling, "c", 1),
    )
    keep, send = call(
        early_sums,
        3,
        [Far((4, 128, COLS)), Far((4, 128, COLS))],
        [],
        ids, *[Far(value) for value in (v0_rows, f0, x1_part, mine, f1)], m2,
    )
    keep, send = call(
        level_three,
        6,
        [(4, 384, COLS), (4, 384, COLS)],
        [(384, S + U2), (384, U3)],
        ids, selector_3, Far(held, 128, 128), Far(f1), Far(w3_columns), Far(keep), Far(send),
        *around(m2),
    )
    w3, keep, send = lax.optimization_barrier((w3, keep, send))
    w3 = around(w3)
    d0, d1, e1, e2, d2, e3, keep, send = call(
        last_level,
        3,
        [(16, COLS), (32, COLS), (16, COLS), (64, COLS), (64, COLS), (192, COLS)]
        + [(4, 128, COLS)] * 2,
        [],
        ids, core_sum(keep, send), Far(v3_rows), *w3,
    )
    (d3,) = call(add_four, 1, [(128, COLS)], [], core_sum(keep, send))
    return d0, d1, e1, d2, e2, d3, e3


def solution(mesh):
    devices = mesh.devices.reshape(2, 2, 2, 4, 2, 4)
    fine = Mesh(devices, ("h", "q", "p", "y", "c", "x"))
    tiled = P(("h", "q", "p", "y", "c"), "x")
    return jax.shard_map(
        shards,
        mesh=fine,
        in_specs=(tiled, tiled, tiled, P(), tiled, tiled, P(), tiled, tiled, P()),
        out_specs=(tiled,) * 7,
        check_vma=False,
    )
```

```python
import jax
import jax.numpy as jnp
from jax import lax
from jax.experimental import pallas as pl
from jax.experimental.pallas import tpu as pltpu
from jax.sharding import Mesh, PartitionSpec as P

S = 1024
BLOCK = 128
U1 = 512
U2 = 1024
U3 = 1536
COLS = 256
F32 = jnp.float32

CORE, PART, SLOT, PAIR, FRONT = 0, 1, 2, 3, 4


def halves(values):
    high = values.astype(jnp.bfloat16)
    return high, (values - high.astype(F32)).astype(jnp.bfloat16)


def dot(left, right, contract=((1,), (0,))):
    left_high, left_low = halves(left)
    right_high, right_low = halves(right)

    def one(a, b):
        return lax.dot_general(a, b, (contract, ((), ())), preferred_element_type=F32)

    return one(left_high, right_high) + (one(left_high, right_low) + one(left_low, right_high))


def inner(left, right):
    return dot(left, right, ((0,), (0,)))


def times(number, unit):
    return pl.multiple_of(number * unit, unit)


def ordered(core, own, other):
    return [jnp.where(core == 0, own, other), jnp.where(core == 0, other, own)]


class Far:

    def __init__(self, value, start=0, rows=None):
        self.value = value
        self.start = start
        self.shape = value if isinstance(value, tuple) else value.shape
        self.shape = (rows or self.shape[0],) + tuple(self.shape[1:])


def call(body, micros, outs, scratch, *operands):
    away_in = [at for at, operand in enumerate(operands) if isinstance(operand, Far)]
    away_out = [at for at, out in enumerate(outs) if isinstance(out, Far)]
    values = [operand.value if isinstance(operand, Far) else operand for operand in operands]
    shapes = [out.value if isinstance(out, Far) else out for out in outs]
    fetched = [operands[at].shape for at in away_in]
    returned = [shapes[at] for at in away_out]
    near = pl.BlockSpec(memory_space=pltpu.VMEM)
    distant = pl.BlockSpec(memory_space=pltpu.HBM)

    def place(at, value):
        if at in away_in:
            return distant
        return near if value.dtype == F32 else pl.BlockSpec(memory_space=pltpu.SMEM)

    def kernel(*refs):
        inputs = list(refs[: len(values)])
        results = list(refs[len(values) : len(values) + len(outs)])
        own = list(refs[len(values) + len(outs) :])
        held = own[: len(scratch)]
        buffers = own[len(scratch) :]
        copies = []
        for number, at in enumerate(away_in):
            rows = pl.ds(operands[at].start, fetched[number][0])
            copy = pltpu.make_async_copy(
                inputs[at].at[rows], buffers[number], buffers[-1].at[number]
            )
            copy.start()
            copies.append(copy)
            inputs[at] = buffers[number]
        for copy in copies:
            copy.wait()
        copies = []
        for number, at in enumerate(away_out):
            number += len(away_in)
            copies.append(
                pltpu.make_async_copy(buffers[number], results[at], buffers[-1].at[number])
            )
            results[at] = buffers[number]
        body(*inputs, *results, *held)
        for copy in copies:
            copy.start()
        for copy in copies:
            copy.wait()

    count = len(fetched) + len(returned)
    return pl.pallas_call(
        kernel,
        out_shape=[jax.ShapeDtypeStruct(shape, F32) for shape in shapes],
        in_specs=[place(at, value) for at, value in enumerate(values)],
        out_specs=[distant if at in away_out else near for at in range(len(outs))],
        scratch_shapes=[pltpu.VMEM(shape, F32) for shape in scratch + fetched + returned]
        + ([pltpu.SemaphoreType.DMA((count,))] if count else []),
        cost_estimate=pl.CostEstimate(
            flops=micros * 1_100_000_000, bytes_accessed=0, transcendentals=0
        ),
        compiler_params=pltpu.CompilerParams(vmem_limit_bytes=(60 if body in (pack,) else 28) * 1024 * 1024),
    )(*values)


def pack(v0, v1, b1, v2, b2, v3, b3, own_1, own_2, own_3, columns_3):
    own_1[0:32, :] = v1[...]
    own_1[32:48, :] = b1[...]
    own_1[48:64, :] = v0[...]
    own_2[0:64, :] = v2[...]
    own_2[64:128, :] = b2[...]
    own_3[0:192, :] = b3[...]
    own_3[192:320, :] = v3[...]
    for copy in range(4):
        columns_3[copy] = v3[...]


def place_ancestors(ids, p0, p1, p2, p3, own_2, pair_2, early, rows, row_0):
    slot, pair = ids[SLOT], ids[PAIR]
    for distance, ref in enumerate((p0, p1, p2, p3)):
        source = slot ^ distance
        values = ref[...]
        rows[pl.ds(256 + times(source, 32), 32), :] = values[0:32]
        rows[pl.ds(384 + times(source, 16), 16), :] = values[48:64]
        row_0[pl.ds(times(source, 16), 16), :] = values[48:64]
        for copy in range(4):
            early[copy, pl.ds(times(source, 32), 32), :] = values[0:32]
            early[copy, pl.ds(256 + times(source, 16), 16), :] = values[32:48]
    for distance, ref in enumerate((own_2, pair_2)):
        start = times(pair ^ distance, 64)
        values = ref[...]
        rows[pl.ds(start, 64), :] = values[64:128]
        rows[pl.ds(128 + start, 64), :] = values[0:64]
        for copy in range(4):
            early[copy, pl.ds(128 + start, 64), :] = values[0:64]


def add(left, right, out):
    out[...] = left[...] + right[...]


def add_four(parts, out):
    out[...] = (parts[0] + parts[1]) + (parts[2] + parts[3])


def couple_front(ids, a0, a1, a2, a3, own, other, w3, v3):
    core, part = ids[CORE], ids[PART]
    total = jnp.zeros((192, COLS), F32)
    for distance, ref in enumerate((a0, a1, a2, a3)):
        quarter = part ^ distance
        total += dot(ref[0:192, :], jnp.concatenate(ordered(core, own[quarter], other[quarter]), 0))
        v3[:, pl.ds(times(quarter, COLS), COLS)] = ref[192:320, :]
    w3[...] = total


def shelve(ids, r0, r1, r2, r3, held):
    for distance, ref in enumerate((r0, r1, r2, r3)):
        held[:, pl.ds(times(ids[PART] ^ distance, COLS), COLS)] = ref[...]


def middle(
    ids, sel, b2, v0_top, h0, h1, h2, h3, own, other, w3, coupling, y1, f0, v0, v1_columns
):
    core, part = ids[CORE], ids[PART]
    v0[0:64, :] = v0_top[...]
    for distance, ref in enumerate((h0, h1, h2, h3)):
        v0[64:128, pl.ds(times(part ^ distance, COLS), COLS)] = ref[...]
    for block in range(4):
        f0[:, block * BLOCK : (block + 1) * BLOCK] = v0[
            :, pl.ds(times(sel[ids[FRONT] >> 2, block], BLOCK), BLOCK)
        ]
    rows = []
    for slot in range(4):
        start = 256 + slot * 16
        for y in range(4):
            rows += ordered(core, own[y, start : start + 16, :], other[y, start : start + 16, :])
    y1[...] = dot(f0[...], jnp.concatenate(rows, 0))
    w2 = jnp.zeros((128, COLS), F32)
    for pair in range(2):
        rows = []
        start = 128 + pair * 64
        for y in range(4):
            rows += ordered(core, own[y, start : start + 64, :], other[y, start : start + 64, :])
        w2 += dot(b2[:, pair * 512 : (pair + 1) * 512], jnp.concatenate(rows, 0))
    for copy in range(4):
        coupling[copy, 0:128, :] = w2
        coupling[copy, 128:320, :] = w3[...]
    for slot in range(4):
        start = slot * 32
        for y in range(4):
            place = slot * 256 + y * 64
            first, second = ordered(
                core, own[y, start : start + 32, :], other[y, start : start + 32, :]
            )
            v1_columns[place : place + 32, :] = first
            v1_columns[place + 32 : place + 64, :] = second


def second_half(ids, y0, y1, y2, y3, v1_columns, m1):
    part = ids[PART]
    total = jnp.zeros((128, COLS), F32)
    for distance, ref in enumerate((y0, y1, y2, y3)):
        total += dot(ref[...], v1_columns[pl.ds(times(part ^ distance, COLS), COLS), :])
    m1[...] = total


def level_two(
    ids, sel, v1, f0, m0, m1, m2, m3, own, other, out, f1, w3_columns, x1_part, mine, x1
):
    core, part, slot = ids[CORE], ids[PART], ids[SLOT]
    x1[0:128, 0:S] = v1[...]
    x1[0:128, S:] = jnp.zeros((128, U1), F32)
    x1[128:256, S:] = f0[...]
    for distance, ref in enumerate((m0, m1, m2, m3)):
        x1[128:256, pl.ds(times(part ^ distance, COLS), COLS)] = -ref[...]
    for block in range(8):
        f1[:, block * BLOCK : (block + 1) * BLOCK] = x1[
            :, pl.ds(times(sel[ids[FRONT] >> 1, block], BLOCK), BLOCK)
        ]
    total = jnp.zeros((256, COLS), F32)
    for pair in range(2):
        rows = []
        for y in range(4):
            start = pair * 64
            rows += ordered(core, own[y, start : start + 64, :], other[y, start : start + 64, :])
        total += dot(f1[:, pair * 512 : (pair + 1) * 512], jnp.concatenate(rows, 0))
    out[...] = total
    for y in range(4):
        first, second = ordered(core, own[y, 128:320, :], other[y, 128:320, :])
        w3_columns[y * 384 : y * 384 + 192, :] = first
        w3_columns[y * 384 + 192 : y * 384 + 384, :] = second
    x1_part[...] = x1[:, pl.ds(times(slot, 256), 256)]
    mine[...] = x1[:, pl.ds(times(part, COLS), COLS)]


def put(core, keep, send, values, start, rows):
    for y in range(4):
        first = values[2 * y * rows : (2 * y + 1) * rows]
        second = values[(2 * y + 1) * rows : (2 * y + 2) * rows]
        keep[y, start : start + rows, :] = jnp.where(core == 0, first, second)
        send[y, start : start + rows, :] = jnp.where(core == 0, second, first)


def early_sums(ids, v0, f0, x1_part, mine, f1, m2, keep, send):
    core, part = ids[CORE], ids[PART]
    front, slot, pair = ids[FRONT], ids[SLOT], ids[PAIR]
    d0 = inner(v0[:, pl.ds(times(front, BLOCK), BLOCK)], v0[:, pl.ds(times(part, COLS), COLS)])
    put(core, keep, send, d0, 0, 16)
    put(core, keep, send, inner(x1_part[...], mine[...]), 16, 32)
    e1 = inner(f0[:, pl.ds(times(slot, BLOCK), BLOCK)], mine[128:256, :])
    put(core, keep, send, e1, 48, 16)
    put(core, keep, send, inner(f1[:, pl.ds(times(pair, 512), 512)], -m2[...]), 64, 64)


def level_three(
    ids, sel, v2, f1, w3_columns, keep_1, send_1, m0, m1, m2, m3, keep, send, x2, f2
):
    core, part, pair = ids[CORE], ids[PART], ids[PAIR]
    x2[0:128, 0:S] = v2[...]
    x2[0:128, S:] = jnp.zeros((128, U2), F32)
    x2[128:384, S:] = f1[...]
    for distance, ref in enumerate((m0, m1, m2, m3)):
        x2[128:384, pl.ds(times(part ^ distance, COLS), COLS)] = -ref[...]
    for block in range(12):
        f2[:, block * BLOCK : (block + 1) * BLOCK] = x2[
            :, pl.ds(times(sel[ids[FRONT], block], BLOCK), BLOCK)
        ]
    total = dot(f2[...], w3_columns[...])
    for y in range(4):
        keep[y, 0:128, :] = keep_1[y]
        send[y, 0:128, :] = send_1[y]
    put(core, keep, send, inner(f2[...], -total), 192, 192)
    mine = x2[:, pl.ds(times(part, COLS), COLS)]
    put(core, keep, send, inner(x2[:, pl.ds(times(pair, 512), 512)], mine), 128, 64)


def last_level(
    ids, parts, v3, w0, w1, w2, w3, d0, d1, e1, e2, d2, e3, keep, send
):
    core, part = ids[CORE], ids[PART]
    total = (parts[0] + parts[1]) + (parts[2] + parts[3])
    d0[...] = total[0:16]
    d1[...] = total[16:48]
    e1[...] = total[48:64]
    e2[...] = total[64:128]
    d2[...] = total[128:192]
    below = total[192:384]
    e3[...] = below
    right = jnp.concatenate([v3[:, pl.ds(times(part, COLS), COLS)], -below], 0)
    for distance, ref in enumerate((w0, w1, w2, w3)):
        place = part ^ distance
        left = jnp.concatenate([v3[:, pl.ds(times(place, COLS), COLS)], ref[...]], 0)
        rows = inner(left, right)
        keep[place] = jnp.where(core == 0, rows[0:128], rows[128:256])
        send[place] = jnp.where(core == 0, rows[128:256], rows[0:128])


def swapped(array, axis, distance, parts=2):
    return lax.ppermute(array, axis, [(i, i ^ distance) for i in range(parts)])


def around(values, axis="x"):
    return [values] + [swapped(values, axis, distance, 4) for distance in (1, 2, 3)]


def exchanged(values):
    return lax.all_to_all(values, "y", 0, 0)


def core_sum(keep, send):
    (total,) = call(add, 1, [keep.shape], [], keep, swapped(send, "c", 1))
    return exchanged(total)


def shards(v0, v1, b1, selector_1, v2, b2, selector_2, v3, b3, selector_3):
    half = lax.axis_index("h")
    quarter = lax.axis_index("q")
    pair = lax.axis_index("p")
    slot = quarter * 2 + pair
    ids = jnp.stack(
        [lax.axis_index("c"), lax.axis_index("x"), slot, pair, half * 4 + slot]
    ).astype(jnp.int32)

    own_1, own_2, own_3, columns_3 = call(
        pack,
        1,
        [(64, COLS), (128, COLS), (320, COLS), (4, 128, COLS)],
        [],
        *[Far(value) for value in (v0, v1, b1, v2, b2, v3, b3)],
    )
    ancestors = around(own_1, ("q", "p"))
    pair_2 = swapped(own_2, "p", 1)
    columns_3 = exchanged(columns_3)
    early, rows, row_0 = call(
        place_ancestors,
        2,
        [(4, 320, COLS), (448, COLS), (64, COLS)],
        [],
        ids, *ancestors, own_2, pair_2,
    )
    early, columns_3 = lax.optimization_barrier((early, columns_3))
    own_rows = around(own_3)
    own_rows, rows = lax.optimization_barrier((own_rows, rows))
    early = exchanged(early)
    row_0 = around(swapped(row_0, "h", 1))
    w3, v3_rows = call(
        couple_front,
        2,
        [(192, COLS), Far((128, S))],
        [],
        ids, *own_rows, columns_3, swapped(columns_3, "c", 1),
    )
    (held,) = call(shelve, 1, [Far((448, S))], [], ids, *around(rows))
    early, row_0, w3, v3_rows, held = lax.optimization_barrier(
        (early, row_0, w3, v3_rows, held)
    )

    coupling, y1, f0, v0_rows, v1_columns = call(
        middle,
        4,
        [(4, 320, COLS), (128, COLS), Far((128, U1)), Far((128, S)), Far((S, COLS))],
        [],
        ids, selector_1, Far(held, 0, 128), Far(held, 384, 64), *row_0,
        early, swapped(early, "c", 1), w3,
    )
    coupling = exchanged(coupling)
    (m1,) = call(second_half, 2, [(128, COLS)], [], ids, *around(y1), Far(v1_columns))
    m1, coupling = lax.optimization_barrier((around(m1), coupling))
    m2, f1, w3_columns, x1_part, mine = call(
        level_two,
        3,
        [(256, COLS), Far((256, U2)), Far((U3, COLS)), Far((256, 256)), Far((256, COLS))],
        [(256, S + U1)],
        ids, selector_2, Far(held, 256, 128), Far(f0), *m1,
        coupling, swapped(coupling, "c", 1),
    )
    keep, send = call(
        early_sums,
        3,
        [Far((4, 128, COLS)), Far((4, 128, COLS))],
        [],
        ids, *[Far(value) for value in (v0_rows, f0, x1_part, mine, f1)], m2,
    )
    keep, send = call(
        level_three,
        6,
        [(4, 384, COLS), (4, 384, COLS)],
        [(384, S + U2), (384, U3)],
        ids, selector_3, Far(held, 128, 128), Far(f1), Far(w3_columns), Far(keep), Far(send),
        *around(m2),
    )
    w3, keep, send = lax.optimization_barrier((w3, keep, send))
    w3 = around(w3)
    d0, d1, e1, e2, d2, e3, keep, send = call(
        last_level,
        3,
        [(16, COLS), (32, COLS), (16, COLS), (64, COLS), (64, COLS), (192, COLS)]
        + [(4, 128, COLS)] * 2,
        [],
        ids, core_sum(keep, send), Far(v3_rows), *w3,
    )
    (d3,) = call(add_four, 1, [(128, COLS)], [], core_sum(keep, send))
    return d0, d1, e1, d2, e2, d3, e3


def solution(mesh):
    devices = mesh.devices.reshape(2, 2, 2, 4, 2, 4)
    fine = Mesh(devices, ("h", "q", "p", "y", "c", "x"))
    tiled = P(("h", "q", "p", "y", "c"), "x")
    return jax.shard_map(
        shards,
        mesh=fine,
        in_specs=(tiled, tiled, tiled, P(), tiled, tiled, P(), tiled, tiled, P()),
        out_specs=(tiled,) * 7,
        check_vma=False,
    )
```

```python
import jax
import jax.numpy as jnp
from jax import lax
from jax.experimental import pallas as pl
from jax.experimental.pallas import tpu as pltpu
from jax.sharding import Mesh, PartitionSpec as P

S = 1024
BLOCK = 128
U1 = 512
U2 = 1024
U3 = 1536
COLS = 256
F32 = jnp.float32

CORE, PART, SLOT, PAIR, FRONT = 0, 1, 2, 3, 4


def halves(values):
    high = values.astype(jnp.bfloat16)
    return high, (values - high.astype(F32)).astype(jnp.bfloat16)


def dot(left, right, contract=((1,), (0,))):
    return from_halves(halves(left), halves(right), contract)


def from_halves(left, right, contract):
    left_high, left_low = left
    right_high, right_low = right

    def one(a, b):
        return lax.dot_general(a, b, (contract, ((), ())), preferred_element_type=F32)

    return one(left_high, right_high) + (one(left_high, right_low) + one(left_low, right_high))


def inner(left, right):
    return dot(left, right, ((0,), (0,)))


def times(number, unit):
    return pl.multiple_of(number * unit, unit)


def ordered(core, own, other):
    return [jnp.where(core == 0, own, other), jnp.where(core == 0, other, own)]


class Far:

    def __init__(self, value, start=0, rows=None):
        self.value = value
        self.start = start
        self.shape = value if isinstance(value, tuple) else value.shape
        self.shape = (rows or self.shape[0],) + tuple(self.shape[1:])


def call(body, micros, outs, scratch, *operands):
    away_in = [at for at, operand in enumerate(operands) if isinstance(operand, Far)]
    away_out = [at for at, out in enumerate(outs) if isinstance(out, Far)]
    values = [operand.value if isinstance(operand, Far) else operand for operand in operands]
    shapes = [out.value if isinstance(out, Far) else out for out in outs]
    fetched = [operands[at].shape for at in away_in]
    returned = [shapes[at] for at in away_out]
    near = pl.BlockSpec(memory_space=pltpu.VMEM)
    distant = pl.BlockSpec(memory_space=pltpu.HBM)

    def place(at, value):
        if at in away_in:
            return distant
        return near if value.dtype == F32 else pl.BlockSpec(memory_space=pltpu.SMEM)

    def kernel(*refs):
        inputs = list(refs[: len(values)])
        results = list(refs[len(values) : len(values) + len(outs)])
        own = list(refs[len(values) + len(outs) :])
        held = own[: len(scratch)]
        buffers = own[len(scratch) :]
        copies = []
        for number, at in enumerate(away_in):
            rows = pl.ds(operands[at].start, fetched[number][0])
            copy = pltpu.make_async_copy(
                inputs[at].at[rows], buffers[number], buffers[-1].at[number]
            )
            copy.start()
            copies.append(copy)
            inputs[at] = buffers[number]
        for copy in copies:
            copy.wait()
        copies = []
        for number, at in enumerate(away_out):
            number += len(away_in)
            copies.append(
                pltpu.make_async_copy(buffers[number], results[at], buffers[-1].at[number])
            )
            results[at] = buffers[number]
        body(*inputs, *results, *held)
        for copy in copies:
            copy.start()
        for copy in copies:
            copy.wait()

    count = len(fetched) + len(returned)
    return pl.pallas_call(
        kernel,
        out_shape=[jax.ShapeDtypeStruct(shape, F32) for shape in shapes],
        in_specs=[place(at, value) for at, value in enumerate(values)],
        out_specs=[distant if at in away_out else near for at in range(len(outs))],
        scratch_shapes=[pltpu.VMEM(shape, F32) for shape in scratch + fetched + returned]
        + ([pltpu.SemaphoreType.DMA((count,))] if count else []),
        cost_estimate=pl.CostEstimate(
            flops=micros * 1_100_000_000, bytes_accessed=0, transcendentals=0
        ),
        compiler_params=pltpu.CompilerParams(vmem_limit_bytes=(60 if body in (pack,) else 28) * 1024 * 1024),
    )(*values)


def pack(v0, v1, b1, v2, b2, v3, b3, own_1, own_2, own_3, columns_3):
    own_1[0:32, :] = v1[...]
    own_1[32:48, :] = b1[...]
    own_1[48:64, :] = v0[...]
    own_2[0:64, :] = v2[...]
    own_2[64:128, :] = b2[...]
    own_3[...] = b3[...]
    for copy in range(4):
        columns_3[copy] = v3[...]


def place_ancestors(ids, p0, p1, p2, p3, own_2, pair_2, early, rows, row_0):
    slot, pair = ids[SLOT], ids[PAIR]
    for distance, ref in enumerate((p0, p1, p2, p3)):
        source = slot ^ distance
        values = ref[...]
        rows[pl.ds(256 + times(source, 32), 32), :] = values[0:32]
        rows[pl.ds(384 + times(source, 16), 16), :] = values[48:64]
        row_0[pl.ds(times(source, 16), 16), :] = values[48:64]
        for copy in range(4):
            early[copy, pl.ds(times(source, 32), 32), :] = values[0:32]
            early[copy, pl.ds(256 + times(source, 16), 16), :] = values[32:48]
    for distance, ref in enumerate((own_2, pair_2)):
        start = times(pair ^ distance, 64)
        values = ref[...]
        rows[pl.ds(start, 64), :] = values[64:128]
        rows[pl.ds(128 + start, 64), :] = values[0:64]
        for copy in range(4):
            early[copy, pl.ds(128 + start, 64), :] = values[0:64]


def add(left, right, out):
    out[...] = left[...] + right[...]


def add_four(parts, out):
    out[...] = (parts[0] + parts[1]) + (parts[2] + parts[3])


def couple_front(ids, a0, a1, a2, a3, v3, own, other, w3, front):
    core, part = ids[CORE], ids[PART]
    total = jnp.zeros((192, COLS), F32)
    for distance, ref in enumerate((a0, a1, a2, a3)):
        quarter = part ^ distance
        total += dot(ref[...], jnp.concatenate(ordered(core, own[quarter], other[quarter]), 0))
    w3[...] = total
    front[0:192, :] = total
    front[192:320, :] = v3[...]


def shelve(ids, r0, r1, r2, r3, held):
    for distance, ref in enumerate((r0, r1, r2, r3)):
        held[:, pl.ds(times(ids[PART] ^ distance, COLS), COLS)] = ref[...]


def middle(
    ids, sel, b2, v0_top, h0, h1, h2, h3, own, other, w3, coupling, y1, f0, v0, v1_columns
):
    core, part = ids[CORE], ids[PART]
    v0[0:64, :] = v0_top[...]
    for distance, ref in enumerate((h0, h1, h2, h3)):
        v0[64:128, pl.ds(times(part ^ distance, COLS), COLS)] = ref[...]
    for block in range(4):
        f0[:, block * BLOCK : (block + 1) * BLOCK] = v0[
            :, pl.ds(times(sel[ids[FRONT] >> 2, block], BLOCK), BLOCK)
        ]
    rows = []
    for slot in range(4):
        start = 256 + slot * 16
        for y in range(4):
            rows += ordered(core, own[y, start : start + 16, :], other[y, start : start + 16, :])
    y1[...] = dot(f0[...], jnp.concatenate(rows, 0))
    w2 = jnp.zeros((128, COLS), F32)
    for pair in range(2):
        rows = []
        start = 128 + pair * 64
        for y in range(4):
            rows += ordered(core, own[y, start : start + 64, :], other[y, start : start + 64, :])
        w2 += dot(b2[:, pair * 512 : (pair + 1) * 512], jnp.concatenate(rows, 0))
    for copy in range(4):
        coupling[copy, 0:128, :] = w2
        coupling[copy, 128:320, :] = w3[...]
    for slot in range(4):
        start = slot * 32
        for y in range(4):
            place = slot * 256 + y * 64
            first, second = ordered(
                core, own[y, start : start + 32, :], other[y, start : start + 32, :]
            )
            v1_columns[place : place + 32, :] = first
            v1_columns[place + 32 : place + 64, :] = second


def second_half(ids, y0, y1, y2, y3, v1_columns, m1):
    part = ids[PART]
    total = jnp.zeros((128, COLS), F32)
    for distance, ref in enumerate((y0, y1, y2, y3)):
        total += dot(ref[...], v1_columns[pl.ds(times(part ^ distance, COLS), COLS), :])
    m1[...] = total


def level_two(
    ids, sel, v1, f0, m0, m1, m2, m3, own, other, out, f1, w3_columns, x1_part, mine, x1
):
    core, part, slot = ids[CORE], ids[PART], ids[SLOT]
    x1[0:128, 0:S] = v1[...]
    x1[0:128, S:] = jnp.zeros((128, U1), F32)
    x1[128:256, S:] = f0[...]
    for distance, ref in enumerate((m0, m1, m2, m3)):
        x1[128:256, pl.ds(times(part ^ distance, COLS), COLS)] = -ref[...]
    for block in range(8):
        f1[:, block * BLOCK : (block + 1) * BLOCK] = x1[
            :, pl.ds(times(sel[ids[FRONT] >> 1, block], BLOCK), BLOCK)
        ]
    total = jnp.zeros((256, COLS), F32)
    for pair in range(2):
        rows = []
        for y in range(4):
            start = pair * 64
            rows += ordered(core, own[y, start : start + 64, :], other[y, start : start + 64, :])
        total += dot(f1[:, pair * 512 : (pair + 1) * 512], jnp.concatenate(rows, 0))
    out[...] = total
    for y in range(4):
        first, second = ordered(core, own[y, 128:320, :], other[y, 128:320, :])
        w3_columns[y * 384 : y * 384 + 192, :] = first
        w3_columns[y * 384 + 192 : y * 384 + 384, :] = second
    x1_part[...] = x1[:, pl.ds(times(slot, 256), 256)]
    mine[...] = x1[:, pl.ds(times(part, COLS), COLS)]


def put(core, keep, send, values, start, rows):
    for y in range(4):
        first = values[2 * y * rows : (2 * y + 1) * rows]
        second = values[(2 * y + 1) * rows : (2 * y + 2) * rows]
        keep[y, start : start + rows, :] = jnp.where(core == 0, first, second)
        send[y, start : start + rows, :] = jnp.where(core == 0, second, first)


def early_sums(ids, v0, f0, x1_part, mine, f1, m2, keep, send):
    core, part = ids[CORE], ids[PART]
    front, slot, pair = ids[FRONT], ids[SLOT], ids[PAIR]
    d0 = inner(v0[:, pl.ds(times(front, BLOCK), BLOCK)], v0[:, pl.ds(times(part, COLS), COLS)])
    put(core, keep, send, d0, 0, 16)
    put(core, keep, send, inner(x1_part[...], mine[...]), 16, 32)
    e1 = inner(f0[:, pl.ds(times(slot, BLOCK), BLOCK)], mine[128:256, :])
    put(core, keep, send, e1, 48, 16)
    put(core, keep, send, inner(f1[:, pl.ds(times(pair, 512), 512)], -m2[...]), 64, 64)


def level_three(
    ids, sel, v2, f1, w3_columns, keep_1, send_1, m0, m1, m2, m3, keep, send, x2, f2
):
    core, part, pair = ids[CORE], ids[PART], ids[PAIR]
    x2[0:128, 0:S] = v2[...]
    x2[0:128, S:] = jnp.zeros((128, U2), F32)
    x2[128:384, S:] = f1[...]
    for distance, ref in enumerate((m0, m1, m2, m3)):
        x2[128:384, pl.ds(times(part ^ distance, COLS), COLS)] = -ref[...]
    for block in range(12):
        f2[:, block * BLOCK : (block + 1) * BLOCK] = x2[
            :, pl.ds(times(sel[ids[FRONT], block], BLOCK), BLOCK)
        ]
    high, low = halves(f2[...])
    total = from_halves((high, low), halves(w3_columns[...]), ((1,), (0,)))
    for y in range(4):
        keep[y, 0:128, :] = keep_1[y]
        send[y, 0:128, :] = send_1[y]
    put(core, keep, send, from_halves((high, low), halves(-total), ((0,), (0,))), 192, 192)
    mine = x2[:, pl.ds(times(part, COLS), COLS)]
    put(core, keep, send, inner(x2[:, pl.ds(times(pair, 512), 512)], mine), 128, 64)


def last_level(
    ids, parts, w0, w1, w2, w3, d0, d1, e1, e2, d2, e3, keep, send
):
    core, part = ids[CORE], ids[PART]
    total = (parts[0] + parts[1]) + (parts[2] + parts[3])
    d0[...] = total[0:16]
    d1[...] = total[16:48]
    e1[...] = total[48:64]
    e2[...] = total[64:128]
    d2[...] = total[128:192]
    below = total[192:384]
    e3[...] = below
    right = jnp.concatenate([-below, w0[192:320, :]], 0)
    for distance, ref in enumerate((w0, w1, w2, w3)):
        place = part ^ distance
        rows = inner(ref[...], right)
        keep[place] = jnp.where(core == 0, rows[0:128], rows[128:256])
        send[place] = jnp.where(core == 0, rows[128:256], rows[0:128])


def swapped(array, axis, distance, parts=2):
    return lax.ppermute(array, axis, [(i, i ^ distance) for i in range(parts)])


def around(values, axis="x"):
    return [values] + [swapped(values, axis, distance, 4) for distance in (1, 2, 3)]


def exchanged(values):
    return lax.all_to_all(values, "y", 0, 0)


def core_sum(keep, send):
    (total,) = call(add, 1, [keep.shape], [], keep, swapped(send, "c", 1))
    return exchanged(total)


def shards(v0, v1, b1, selector_1, v2, b2, selector_2, v3, b3, selector_3):
    half = lax.axis_index("h")
    quarter = lax.axis_index("q")
    pair = lax.axis_index("p")
    slot = quarter * 2 + pair
    ids = jnp.stack(
        [lax.axis_index("c"), lax.axis_index("x"), slot, pair, half * 4 + slot]
    ).astype(jnp.int32)

    own_1, own_2, own_3, columns_3 = call(
        pack,
        1,
        [(64, COLS), (128, COLS), (192, COLS), (4, 128, COLS)],
        [],
        *[Far(value) for value in (v0, v1, b1, v2, b2, v3, b3)],
    )
    ancestors = around(own_1, ("q", "p"))
    pair_2 = swapped(own_2, "p", 1)
    columns_3 = exchanged(columns_3)
    early, rows, row_0 = call(
        place_ancestors,
        2,
        [(4, 320, COLS), (448, COLS), (64, COLS)],
        [],
        ids, Far(ancestors[0]), *ancestors[1:], Far(own_2), pair_2,
    )
    own_rows = around(own_3)
    early, columns_3, own_rows, rows = lax.optimization_barrier(
        (early, columns_3, own_rows, rows)
    )
    early = exchanged(early)
    row_0 = around(swapped(row_0, "h", 1))
    w3, front = call(
        couple_front,
        2,
        [(192, COLS), (320, COLS)],
        [],
        ids, *own_rows, Far(v3), columns_3, swapped(columns_3, "c", 1),
    )
    (held,) = call(shelve, 1, [Far((448, S))], [], ids, *around(rows))
    early, row_0, w3, front, held = lax.optimization_barrier((early, row_0, w3, front, held))

    coupling, y1, f0, v0_rows, v1_columns = call(
        middle,
        4,
        [(4, 320, COLS), (128, COLS), Far((128, U1)), Far((128, S)), Far((S, COLS))],
        [],
        ids, selector_1, Far(held, 0, 128), Far(held, 384, 64), *row_0,
        early, swapped(early, "c", 1), w3,
    )
    coupling = exchanged(coupling)
    (m1,) = call(second_half, 2, [(128, COLS)], [], ids, *around(y1), Far(v1_columns))
    m1, coupling = lax.optimization_barrier((around(m1), coupling))
    m2, f1, w3_columns, x1_part, mine = call(
        level_two,
        3,
        [(256, COLS), Far((256, U2)), Far((U3, COLS)), Far((256, 256)), Far((256, COLS))],
        [(256, S + U1)],
        ids, selector_2, Far(held, 256, 128), Far(f0), *m1,
        coupling, swapped(coupling, "c", 1),
    )
    keep, send = call(
        early_sums,
        3,
        [Far((4, 128, COLS)), Far((4, 128, COLS))],
        [],
        ids, *[Far(value) for value in (v0_rows, f0, x1_part, mine, f1)], m2,
    )
    keep, send = call(
        level_three,
        6,
        [(4, 384, COLS), (4, 384, COLS)],
        [(384, S + U2), (384, U3)],
        ids, selector_3, Far(held, 128, 128), Far(f1), Far(w3_columns), Far(keep), Far(send),
        *around(m2),
    )
    front, keep, send = lax.optimization_barrier((front, keep, send))
    d0, d1, e1, e2, d2, e3, keep, send = call(
        last_level,
        3,
        [(16, COLS), (32, COLS), (16, COLS), (64, COLS), (64, COLS), (192, COLS)]
        + [(4, 128, COLS)] * 2,
        [],
        ids, core_sum(keep, send), *around(front),
    )
    (d3,) = call(add_four, 1, [(128, COLS)], [], core_sum(keep, send))
    return d0, d1, e1, d2, e2, d3, e3


def solution(mesh):
    devices = mesh.devices.reshape(2, 2, 2, 4, 2, 4)
    fine = Mesh(devices, ("h", "q", "p", "y", "c", "x"))
    tiled = P(("h", "q", "p", "y", "c"), "x")
    return jax.shard_map(
        shards,
        mesh=fine,
        in_specs=(tiled, tiled, tiled, P(), tiled, tiled, P(), tiled, tiled, P()),
        out_specs=(tiled,) * 7,
        check_vma=False,
    )
```

```python
import jax
import jax.numpy as jnp
from jax import lax
from jax.experimental import pallas as pl
from jax.experimental.pallas import tpu as pltpu
from jax.sharding import Mesh, PartitionSpec as P

S = 1024
BLOCK = 128
U1 = 512
U2 = 1024
U3 = 1536
COLS = 256
F32 = jnp.float32

CORE, PART, SLOT, PAIR, FRONT = 0, 1, 2, 3, 4


def halves(values):
    high = values.astype(jnp.bfloat16)
    return high, (values - high.astype(F32)).astype(jnp.bfloat16)


def dot(left, right, contract=((1,), (0,))):
    return from_halves(halves(left), halves(right), contract)


def from_halves(left, right, contract):
    left_high, left_low = left
    right_high, right_low = right

    def one(a, b):
        return lax.dot_general(a, b, (contract, ((), ())), preferred_element_type=F32)

    return one(left_high, right_high) + (one(left_high, right_low) + one(left_low, right_high))


def inner(left, right):
    return dot(left, right, ((0,), (0,)))


def times(number, unit):
    return pl.multiple_of(number * unit, unit)


def ordered(core, own, other):
    return [jnp.where(core == 0, own, other), jnp.where(core == 0, other, own)]


class Far:

    def __init__(self, value, start=0, rows=None):
        self.value = value
        self.start = start
        self.shape = value if isinstance(value, tuple) else value.shape
        self.shape = (rows or self.shape[0],) + tuple(self.shape[1:])


def call(body, micros, outs, scratch, *operands):
    away_in = [at for at, operand in enumerate(operands) if isinstance(operand, Far)]
    away_out = [at for at, out in enumerate(outs) if isinstance(out, Far)]
    values = [operand.value if isinstance(operand, Far) else operand for operand in operands]
    shapes = [out.value if isinstance(out, Far) else out for out in outs]
    fetched = [operands[at].shape for at in away_in]
    returned = [shapes[at] for at in away_out]
    near = pl.BlockSpec(memory_space=pltpu.VMEM)
    distant = pl.BlockSpec(memory_space=pltpu.HBM)

    def place(at, value):
        if at in away_in:
            return distant
        return near if value.dtype == F32 else pl.BlockSpec(memory_space=pltpu.SMEM)

    def kernel(*refs):
        inputs = list(refs[: len(values)])
        results = list(refs[len(values) : len(values) + len(outs)])
        own = list(refs[len(values) + len(outs) :])
        held = own[: len(scratch)]
        buffers = own[len(scratch) :]
        copies = []
        for number, at in enumerate(away_in):
            rows = pl.ds(operands[at].start, fetched[number][0])
            copy = pltpu.make_async_copy(
                inputs[at].at[rows], buffers[number], buffers[-1].at[number]
            )
            copy.start()
            copies.append(copy)
            inputs[at] = buffers[number]
        for copy in copies:
            copy.wait()
        copies = []
        for number, at in enumerate(away_out):
            number += len(away_in)
            copies.append(
                pltpu.make_async_copy(buffers[number], results[at], buffers[-1].at[number])
            )
            results[at] = buffers[number]
        body(*inputs, *results, *held)
        for copy in copies:
            copy.start()
        for copy in copies:
            copy.wait()

    count = len(fetched) + len(returned)
    return pl.pallas_call(
        kernel,
        out_shape=[jax.ShapeDtypeStruct(shape, F32) for shape in shapes],
        in_specs=[place(at, value) for at, value in enumerate(values)],
        out_specs=[distant if at in away_out else near for at in range(len(outs))],
        scratch_shapes=[pltpu.VMEM(shape, F32) for shape in scratch + fetched + returned]
        + ([pltpu.SemaphoreType.DMA((count,))] if count else []),
        cost_estimate=pl.CostEstimate(
            flops=micros * 1_100_000_000, bytes_accessed=0, transcendentals=0
        ),
        compiler_params=pltpu.CompilerParams(vmem_limit_bytes=(60 if body in (pack,) else 28) * 1024 * 1024),
    )(*values)


def pack(v0, v1, b1, v2, b2, v3, b3, own_1, own_2, own_3, columns_3):
    own_1[0:32, :] = v1[...]
    own_1[32:48, :] = b1[...]
    own_1[48:64, :] = v0[...]
    own_2[0:64, :] = v2[...]
    own_2[64:128, :] = b2[...]
    own_3[...] = b3[...]
    for copy in range(4):
        columns_3[copy] = v3[...]


def place_ancestors(ids, p0, p1, p2, p3, own_2, pair_2, early, rows, row_0):
    slot, pair = ids[SLOT], ids[PAIR]
    for distance, ref in enumerate((p0, p1, p2, p3)):
        source = slot ^ distance
        values = ref[...]
        rows[pl.ds(256 + times(source, 32), 32), :] = values[0:32]
        rows[pl.ds(384 + times(source, 16), 16), :] = values[48:64]
        row_0[pl.ds(times(source, 16), 16), :] = values[48:64]
        for copy in range(4):
            early[copy, pl.ds(times(source, 32), 32), :] = values[0:32]
            early[copy, pl.ds(256 + times(source, 16), 16), :] = values[32:48]
    for distance, ref in enumerate((own_2, pair_2)):
        start = times(pair ^ distance, 64)
        values = ref[...]
        rows[pl.ds(start, 64), :] = values[64:128]
        rows[pl.ds(128 + start, 64), :] = values[0:64]
        for copy in range(4):
            early[copy, pl.ds(128 + start, 64), :] = values[0:64]


def add(left, right, out):
    out[...] = left[...] + right[...]


def add_four(parts, out):
    out[...] = (parts[0] + parts[1]) + (parts[2] + parts[3])


def couple_front(ids, a0, a1, a2, a3, v3, own, other, w3, front):
    core, part = ids[CORE], ids[PART]
    total = jnp.zeros((192, COLS), F32)
    for distance, ref in enumerate((a0, a1, a2, a3)):
        quarter = part ^ distance
        total += dot(ref[...], jnp.concatenate(ordered(core, own[quarter], other[quarter]), 0))
    w3[...] = total
    front[0:192, :] = total
    front[192:320, :] = v3[...]


def shelve(ids, r0, r1, r2, r3, held):
    for distance, ref in enumerate((r0, r1, r2, r3)):
        held[:, pl.ds(times(ids[PART] ^ distance, COLS), COLS)] = ref[...]


def middle(
    ids, sel, b2, v0_top, h0, h1, h2, h3, own, other, w3, coupling, y1, f0, v0, v1_columns
):
    core, part = ids[CORE], ids[PART]
    v0[0:64, :] = v0_top[...]
    for distance, ref in enumerate((h0, h1, h2, h3)):
        v0[64:128, pl.ds(times(part ^ distance, COLS), COLS)] = ref[...]
    for block in range(4):
        f0[:, block * BLOCK : (block + 1) * BLOCK] = v0[
            :, pl.ds(times(sel[ids[FRONT] >> 2, block], BLOCK), BLOCK)
        ]
    rows = []
    for slot in range(4):
        start = 256 + slot * 16
        for y in range(4):
            rows += ordered(core, own[y, start : start + 16, :], other[y, start : start + 16, :])
    y1[...] = dot(f0[...], jnp.concatenate(rows, 0))
    w2 = jnp.zeros((128, COLS), F32)
    for pair in range(2):
        rows = []
        start = 128 + pair * 64
        for y in range(4):
            rows += ordered(core, own[y, start : start + 64, :], other[y, start : start + 64, :])
        w2 += dot(b2[:, pair * 512 : (pair + 1) * 512], jnp.concatenate(rows, 0))
    for copy in range(4):
        coupling[copy, 0:128, :] = w2
        coupling[copy, 128:320, :] = w3[...]
    for slot in range(4):
        start = slot * 32
        for y in range(4):
            place = slot * 256 + y * 64
            first, second = ordered(
                core, own[y, start : start + 32, :], other[y, start : start + 32, :]
            )
            v1_columns[place : place + 32, :] = first
            v1_columns[place + 32 : place + 64, :] = second


def second_half(ids, y0, y1, y2, y3, v1_columns, m1):
    part = ids[PART]
    total = jnp.zeros((128, COLS), F32)
    for distance, ref in enumerate((y0, y1, y2, y3)):
        total += dot(ref[...], v1_columns[pl.ds(times(part ^ distance, COLS), COLS), :])
    m1[...] = total


def level_two(
    ids, sel, v1, f0, m0, m1, m2, m3, own, other, out, f1, w3_columns, x1_part, mine, x1
):
    core, part, slot = ids[CORE], ids[PART], ids[SLOT]
    x1[0:128, 0:S] = v1[...]
    x1[0:128, S:] = jnp.zeros((128, U1), F32)
    x1[128:256, S:] = f0[...]
    for distance, ref in enumerate((m0, m1, m2, m3)):
        x1[128:256, pl.ds(times(part ^ distance, COLS), COLS)] = -ref[...]
    for block in range(8):
        f1[:, block * BLOCK : (block + 1) * BLOCK] = x1[
            :, pl.ds(times(sel[ids[FRONT] >> 1, block], BLOCK), BLOCK)
        ]
    total = jnp.zeros((256, COLS), F32)
    for pair in range(2):
        rows = []
        for y in range(4):
            start = pair * 64
            rows += ordered(core, own[y, start : start + 64, :], other[y, start : start + 64, :])
        total += dot(f1[:, pair * 512 : (pair + 1) * 512], jnp.concatenate(rows, 0))
    out[...] = total
    for y in range(4):
        first, second = ordered(core, own[y, 128:320, :], other[y, 128:320, :])
        w3_columns[y * 384 : y * 384 + 192, :] = first
        w3_columns[y * 384 + 192 : y * 384 + 384, :] = second
    x1_part[...] = x1[:, pl.ds(times(slot, 256), 256)]
    mine[...] = x1[:, pl.ds(times(part, COLS), COLS)]


def put(core, keep, send, values, start, rows):
    for y in range(4):
        first = values[2 * y * rows : (2 * y + 1) * rows]
        second = values[(2 * y + 1) * rows : (2 * y + 2) * rows]
        keep[y, start : start + rows, :] = jnp.where(core == 0, first, second)
        send[y, start : start + rows, :] = jnp.where(core == 0, second, first)


def early_sums(ids, v0, f0, x1_part, mine, f1, m2, keep, send):
    core, part = ids[CORE], ids[PART]
    front, slot, pair = ids[FRONT], ids[SLOT], ids[PAIR]
    d0 = inner(v0[:, pl.ds(times(front, BLOCK), BLOCK)], v0[:, pl.ds(times(part, COLS), COLS)])
    put(core, keep, send, d0, 0, 16)
    put(core, keep, send, inner(x1_part[...], mine[...]), 16, 32)
    e1 = inner(f0[:, pl.ds(times(slot, BLOCK), BLOCK)], mine[128:256, :])
    put(core, keep, send, e1, 48, 16)
    put(core, keep, send, inner(f1[:, pl.ds(times(pair, 512), 512)], -m2[...]), 64, 64)


def level_three(
    ids, sel, v2, f1, w3_columns, keep_1, send_1, m0, m1, m2, m3, keep, send, x2, f2
):
    core, part, pair = ids[CORE], ids[PART], ids[PAIR]
    x2[0:128, 0:S] = v2[...]
    x2[0:128, S:] = jnp.zeros((128, U2), F32)
    x2[128:384, S:] = f1[...]
    for distance, ref in enumerate((m0, m1, m2, m3)):
        x2[128:384, pl.ds(times(part ^ distance, COLS), COLS)] = -ref[...]
    for block in range(12):
        f2[:, block * BLOCK : (block + 1) * BLOCK] = x2[
            :, pl.ds(times(sel[ids[FRONT], block], BLOCK), BLOCK)
        ]
    high, low = halves(f2[...])
    total = from_halves((high, low), halves(w3_columns[...]), ((1,), (0,)))
    for y in range(4):
        keep[y, 0:128, :] = keep_1[y]
        send[y, 0:128, :] = send_1[y]
    put(core, keep, send, from_halves((high, low), halves(-total), ((0,), (0,))), 192, 192)
    mine = x2[:, pl.ds(times(part, COLS), COLS)]
    put(core, keep, send, inner(x2[:, pl.ds(times(pair, 512), 512)], mine), 128, 64)


def last_level(
    ids, parts, w0, w1, w2, w3, d0, d1, e1, e2, d2, e3, keep, send
):
    core, part = ids[CORE], ids[PART]
    total = (parts[0] + parts[1]) + (parts[2] + parts[3])
    d0[...] = total[0:16]
    d1[...] = total[16:48]
    e1[...] = total[48:64]
    e2[...] = total[64:128]
    d2[...] = total[128:192]
    below = total[192:384]
    e3[...] = below
    right = jnp.concatenate([-below, w0[192:320, :]], 0)
    for distance, ref in enumerate((w0, w1, w2, w3)):
        place = part ^ distance
        rows = inner(ref[...], right)
        keep[place] = jnp.where(core == 0, rows[0:128], rows[128:256])
        send[place] = jnp.where(core == 0, rows[128:256], rows[0:128])


def swapped(array, axis, distance, parts=2):
    return lax.ppermute(array, axis, [(i, i ^ distance) for i in range(parts)])


def around(values, axis="x"):
    return [values] + [swapped(values, axis, distance, 4) for distance in (1, 2, 3)]


def exchanged(values):
    return lax.all_to_all(values, "y", 0, 0)


def core_sum(keep, send):
    (total,) = call(add, 1, [keep.shape], [], keep, swapped(send, "c", 1))
    return exchanged(total)


def shards(v0, v1, b1, selector_1, v2, b2, selector_2, v3, b3, selector_3):
    half = lax.axis_index("h")
    quarter = lax.axis_index("q")
    pair = lax.axis_index("p")
    slot = quarter * 2 + pair
    ids = jnp.stack(
        [lax.axis_index("c"), lax.axis_index("x"), slot, pair, half * 4 + slot]
    ).astype(jnp.int32)

    own_1, own_2, own_3, columns_3 = call(
        pack,
        1,
        [(64, COLS), (128, COLS), (192, COLS), (4, 128, COLS)],
        [],
        *[Far(value) for value in (v0, v1, b1, v2, b2, v3, b3)],
    )
    ancestors = around(own_1, ("q", "p"))
    pair_2 = swapped(own_2, "p", 1)
    columns_3 = exchanged(columns_3)
    early, rows, row_0 = call(
        place_ancestors,
        2,
        [(4, 320, COLS), (448, COLS), (64, COLS)],
        [],
        ids, Far(ancestors[0]), *ancestors[1:], Far(own_2), pair_2,
    )
    own_rows = around(own_3)
    early, columns_3, own_rows, rows = lax.optimization_barrier(
        (early, columns_3, own_rows, rows)
    )
    early = exchanged(early)
    row_0 = around(swapped(row_0, "h", 1))
    w3, front = call(
        couple_front,
        2,
        [(192, COLS), (320, COLS)],
        [],
        ids, *own_rows, Far(v3), columns_3, swapped(columns_3, "c", 1),
    )
    (held,) = call(shelve, 1, [Far((448, S))], [], ids, *around(rows))
    early, row_0, w3, front, held = lax.optimization_barrier((early, row_0, w3, front, held))

    coupling, y1, f0, v0_rows, v1_columns = call(
        middle,
        4,
        [(4, 320, COLS), (128, COLS), Far((128, U1)), Far((128, S)), Far((S, COLS))],
        [],
        ids, selector_1, Far(held, 0, 128), Far(held, 384, 64), *row_0,
        early, swapped(early, "c", 1), w3,
    )
    coupling = exchanged(coupling)
    (m1,) = call(second_half, 2, [(128, COLS)], [], ids, *around(y1), Far(v1_columns))
    m1, coupling = lax.optimization_barrier((around(m1), coupling))
    m2, f1, w3_columns, x1_part, mine = call(
        level_two,
        3,
        [(256, COLS), Far((256, U2)), Far((U3, COLS)), (256, 256), (256, COLS)],
        [(256, S + U1)],
        ids, selector_2, Far(held, 256, 128), Far(f0), *m1,
        coupling, swapped(coupling, "c", 1),
    )
    keep, send = call(
        early_sums,
        3,
        [(4, 128, COLS), (4, 128, COLS)],
        [],
        ids, Far(v0_rows), Far(f0), x1_part, mine, Far(f1), m2,
    )
    keep, send = call(
        level_three,
        6,
        [(4, 384, COLS), (4, 384, COLS)],
        [(384, S + U2), (384, U3)],
        ids, selector_3, Far(held, 128, 128), Far(f1), Far(w3_columns), keep, send,
        *around(m2),
    )
    front, keep, send = lax.optimization_barrier((front, keep, send))
    d0, d1, e1, e2, d2, e3, keep, send = call(
        last_level,
        3,
        [(16, COLS), (32, COLS), (16, COLS), (64, COLS), (64, COLS), (192, COLS)]
        + [(4, 128, COLS)] * 2,
        [],
        ids, core_sum(keep, send), *around(front),
    )
    (d3,) = call(add_four, 1, [(128, COLS)], [], core_sum(keep, send))
    return d0, d1, e1, d2, e2, d3, e3


def solution(mesh):
    devices = mesh.devices.reshape(2, 2, 2, 4, 2, 4)
    fine = Mesh(devices, ("h", "q", "p", "y", "c", "x"))
    tiled = P(("h", "q", "p", "y", "c"), "x")
    return jax.shard_map(
        shards,
        mesh=fine,
        in_specs=(tiled, tiled, tiled, P(), tiled, tiled, P(), tiled, tiled, P()),
        out_specs=(tiled,) * 7,
        check_vma=False,
    )
```
